32 devices in a mesh: sensor: 4 (over z), channel: 4 (over y, x), tm: 2 (over core).
Axes of the slice: x: 2, y: 2, z: 4, core: 2. Of those that a mesh axis runs over, the one named last changes fastest.
Arguments:
- tensor: float32 [3072, 128, 512], P('sensor', 'tm', 'channel'), may hold values from -6 to 6
- core: float32 [64, 64, 32], replicated, may hold values from -0.015625 to 0.015625
- sensor_factor: float32 [3072, 64], P('sensor'), may hold values from -6 to 6
- channel_factor: float32 [512, 64], P('channel'), may hold values from -6 to 6
- time_factor: float32 [128, 32], P('tm'), may hold values from -6 to 6
- neighbour_ids: int32 [24, 4], P('sensor'), may hold values from 0 to 23
- edge_weights: int32 [24, 4, 128, 128], P('sensor'), may hold values from 0 to 3
Outputs:
- core_grad: float32 [64, 64, 32], replicated
- sensor_grad: float32 [3072, 64], P(('sensor', 'channel', 'tm'))
- channel_grad: float32 [512, 64], P('channel')
- time_grad: float32 [128, 32], P('tm')
The draws below stay inside these ranges and needn't reach their ends.
All inputs are finite; a program needn't handle non-finite values.
Results may differ from the reference program's by a relative error of at most 0.0001.
Values sent between devices are 32-bit elements; how exact they have to be, the bound alone decides.
No kernel may reach another device: no remote copies, remote signals or barrier semaphores. Data moves between devices by JAX's collectives and lax.ppermute only.
A program may use at most 192 MiB of HBM per device.

```python
import math
import jax
import jax.numpy as jnp
from jax import lax

CHANNELS = 512
R1 = 64
R2 = 64
R3 = 32
BLOCK = 128
NBR = 4
SENSORS = 3072
TIME = 128
BLOCKS = 24


def plant(array, own_key, low, top_value):
    longest = array.shape.index(max(array.shape))
    spots = []
    for shift in (0, 1):
        where = [jax.random.randint(jax.random.fold_in(own_key, axis), (), 0, length) for axis, length in enumerate(array.shape)]
        where[longest] = (where[longest] + shift) % array.shape[longest]
        spots.append(tuple(where))
    return array.at[spots[0]].set(low).at[spots[1]].set(top_value)


def shard_levels(rng, shape, cuts, low, top_value):
    def one(axis_at, shards_of):
        draws = jax.random.uniform(jax.random.fold_in(jax.random.fold_in(rng, 6), axis_at), (shards_of,), jnp.float32, low / len(cuts), top_value / len(cuts))
        return jnp.repeat(jnp.exp(draws), shape[axis_at] // shards_of).reshape((-1,) + (1,) * (len(shape) - axis_at - 1))

    level = one(*cuts[0])
    for cut in cuts[1:]:
        level = level * one(*cut)
    return level


def scatter_about(rng, shape, spread, reach, shards=(), kind=jnp.bfloat16):
    level = shard_levels(rng, shape, shards, -0.22, 0.18) if shards else 1.0
    result = jax.random.normal(rng, shape, jnp.float32) * spread * level
    return jnp.minimum(jnp.maximum(result, -reach), reach).astype(kind)


def setup_inputs(seed: int = 0) -> dict:
    keys = jax.random.split(jax.random.key(seed), 8)
    return {
        "tensor": scatter_about(keys[0], (SENSORS, TIME, CHANNELS), 1.0, 6.0, ((0, 4), (1, 2), (2, 4)), jnp.float32),
        "core": scatter_about(keys[1], (R1, R2, R3), (R1 * R2 * R3) ** -0.5, 0.015625, (), jnp.float32),
        "sensor_factor": scatter_about(keys[2], (SENSORS, R1), 1.0, 6.0, ((0, 4),), jnp.float32),
        "channel_factor": scatter_about(keys[3], (CHANNELS, R2), 1.0, 6.0, ((0, 4),), jnp.float32),
        "time_factor": scatter_about(keys[4], (TIME, R3), 1.0, 6.0, ((0, 2),), jnp.float32),
        "neighbour_ids": plant(jax.random.randint(keys[5], (BLOCKS, NBR), 0, BLOCKS), jax.random.fold_in(keys[5], 1), 0, BLOCKS - 1).astype(jnp.int32),
        "edge_weights": plant(jax.random.randint(keys[6], (BLOCKS, NBR, BLOCK, BLOCK), 0, 4), jax.random.fold_in(keys[6], 1), 0, 3).astype(jnp.int32),
    }


lap_weight = 1.0 / 512.0
highest = lax.Precision.HIGHEST

def reference(tensor, core, sensor_factor, channel_factor, time_factor, neighbour_ids, edge_weights):
    core_time = jnp.einsum('rst,kt->rks', core, time_factor, precision=highest)
    core_both = jnp.einsum('rks,js->rkj', core_time, channel_factor, precision=highest)
    core_chan = jnp.einsum('rst,js->rtj', core, channel_factor, precision=highest)
    flat_core = core_both.reshape(R1, TIME * CHANNELS)

    def accumulate(running, pieces):
        tensor_block, factor_block = pieces
        residual = jnp.dot(factor_block, flat_core, precision=highest) - tensor_block.reshape(BLOCK, TIME * CHANNELS)
        folded = jnp.dot(factor_block.T, residual, precision=highest)
        fit_block = jnp.dot(residual, flat_core.T, precision=highest)
        return (running + folded, fit_block)
    start = jnp.zeros((R1, TIME * CHANNELS), jnp.float32)
    folded_total, fit_rows = lax.scan(accumulate, start, (tensor.reshape(BLOCKS, BLOCK, TIME, CHANNELS), sensor_factor.reshape(BLOCKS, BLOCK, R1)))
    folded3 = folded_total.reshape(R1, TIME, CHANNELS)
    inner = jnp.einsum('rkj,js->rks', folded3, channel_factor, precision=highest)
    core_grad = jnp.einsum('rks,kt->rst', inner, time_factor, precision=highest) / math.sqrt(SENSORS * TIME * CHANNELS)
    channel_grad = jnp.einsum('rkj,rks->js', folded3, core_time, precision=highest) / math.sqrt(SENSORS * TIME)
    time_grad = jnp.einsum('rkj,rtj->kt', folded3, core_chan, precision=highest) / math.sqrt(SENSORS * CHANNELS)
    fit = fit_rows.reshape(SENSORS, R1) / math.sqrt(TIME * CHANNELS)
    weights_float = edge_weights.astype(jnp.float32)
    blocks_all = sensor_factor.reshape(BLOCKS, BLOCK, R1)
    neighbours = blocks_all[neighbour_ids]
    pulled = jnp.einsum('bnic,bncd->bid', weights_float, neighbours, precision=highest)
    degree = lax.optimization_barrier(jnp.sum(weights_float, axis=(1, 3)))
    graph_term = lap_weight * (degree[:, :, None] * blocks_all - pulled)
    sensor_grad = fit + graph_term.reshape(SENSORS, R1)
    return (core_grad, sensor_grad, channel_grad, time_grad)
```

```python
import functools
import math

import jax
import jax.numpy as jnp
from jax import lax
from jax.experimental import pallas as pl
from jax.experimental.pallas import tpu as pltpu
from jax.sharding import PartitionSpec as P

lap_weight = 1.0 / 512.0
f32, bf16 = jnp.float32, jnp.bfloat16
NN = (((1,), (0,)), ((), ()))
NT = (((1,), (1,)), ((), ()))
TN = (((0,), (0,)), ((), ()))
LANES = 128
vmem = pl.BlockSpec(memory_space=pltpu.VMEM)
smem = pl.BlockSpec(memory_space=pltpu.SMEM)
anywhere = pl.BlockSpec(memory_space=pl.ANY)


def split(x):
    high = x.astype(bf16)
    return high, (x - high.astype(f32)).astype(bf16)


def dot(a, b, dims=NN):
    return lax.dot_general(a, b, dims, preferred_element_type=f32)


def dot3(a, b, dims=NN):
    return dot(a[0], b[0], dims) + (dot(a[0], b[1], dims) + dot(a[1], b[0], dims))


def halves(x):
    w = x.shape[1] // 2
    return jnp.concatenate([x[:, :w], x[:, w:]], axis=0)


def paired(x):
    n = x.shape[0] // 2
    return jnp.concatenate([x[:n], x[n:]], axis=1)


class Plan:
    def __init__(self, tensor, core, n_sensor, n_channel, n_time):
        self.sensors, self.times, self.chans = tensor
        self.r1, self.r2, self.r3 = core
        self.n_sensor, self.n_channel, self.n_time = n_sensor, n_channel, n_time
        self.parts = n_channel * n_time
        self.pairs = self.r1 // 2
        self.pairs_part = self.pairs // self.parts
        self.core_rows = self.pairs_part * self.r3
        self.time_rows = self.r3 // n_channel
        self.share = self.sensors // self.parts
        self.fit_rows = self.share // 2
        self.chunk = self.core_rows + self.time_rows + self.fit_rows
        self.sum_rows = self.core_rows + self.time_rows
        self.chan_rows = self.r2 // n_time
        self.rows = n_channel * self.chunk + self.chan_rows
        total = (self.sensors * n_sensor, self.times * n_time, self.chans * n_channel)
        self.core_scale = 1.0 / math.sqrt(total[0] * total[1] * total[2])
        self.chan_scale = 1.0 / math.sqrt(total[0] * total[1])
        self.time_scale = 1.0 / math.sqrt(total[0] * total[2])
        self.fit_scale = 1.0 / math.sqrt(total[1] * total[2])


def partial_kernel(
    p, wide, slots, tall,
    place, x_hbm, core, sensor_t, chan_t, time_t, keep, send,
    buf, sem, core_pair, ct, inner_ref, fit_acc, chan_acc, time_acc, ggt, sensor_s,
):
    r1, r2, r3 = p.r1, p.r2, p.r3
    width = wide * p.chans
    steps = p.times // wide
    my_time, my_chan = place[0], place[1]

    def copies(step, slot):
        return [
            pltpu.make_async_copy(
                x_hbm.at[:, step * wide + h, :],
                buf.at[slot, :, h * p.chans : (h + 1) * p.chans],
                sem.at[slot, h],
            )
            for h in range(wide)
        ]

    for s in range(slots):
        for c in copies(s, s):
            c.start()

    time_s = split(time_t[...])
    for r in range(p.pairs):
        pair = jnp.concatenate([core[r], core[r + p.pairs]], axis=1)
        core_pair[r] = pair
        ct[r * p.times : (r + 1) * p.times, :] = dot3(time_s, split(pair), TN)
    chan_s = split(chan_t[...])
    chan_rows = chan_t[...].T
    chan_rows_s = split(chan_rows)
    sensor_f = sensor_t[...]
    sensor_h, sensor_l = split(sensor_f)
    sensor_s[0:r1, :] = sensor_h
    sensor_s[r1 : 2 * r1, :] = sensor_l
    gram_s = split(dot3((sensor_h, sensor_l), (sensor_h, sensor_l), NT))
    fit_acc[...] = jnp.zeros_like(fit_acc)
    chan_acc[...] = jnp.zeros_like(chan_acc)
    ggt[...] = jnp.zeros_like(ggt)

    def one(step, slot):
        ks = [step * wide + h for h in range(wide)]
        ct_rows = jnp.concatenate(
            [halves(ct[pl.ds(k, p.pairs, stride=p.times), :]) for k in ks], axis=0
        )
        ct_s = split(ct_rows)
        g = dot3(ct_s, chan_s)
        g_wide = jnp.concatenate([g[h * r1 : (h + 1) * r1] for h in range(wide)], axis=1)
        gw_s = split(g_wide)
        ggt[...] += dot3(gw_s, gw_s, NT)
        gt_h, gt_l = split(g.T)
        g_both = jnp.concatenate(
            [
                jnp.concatenate([gt_h[:, h * r1 : (h + 1) * r1], gt_l[:, h * r1 : (h + 1) * r1]], axis=1)
                for h in range(wide)
            ],
            axis=0,
        )
        g_high = jnp.concatenate([gt_h[:, h * r1 : (h + 1) * r1] for h in range(wide)], axis=0)
        for c in copies(step, slot):
            c.wait()
        folded = dot3(gram_s, gw_s)
        for i in range(0, p.sensors, tall):
            x_h, x_l = split(buf[slot, i : i + tall, :])
            f = dot(x_h, g_both)
            fit_acc[i : i + tall, :] += f[:, :r1] + f[:, r1:] + dot(x_l, g_high)
            a = dot(sensor_s[:, i : i + tall], x_h)
            folded = folded - (a[:r1] + a[r1:] + dot(sensor_s[0:r1, i : i + tall], x_l))
        f_rows = jnp.concatenate(
            [folded[:, h * p.chans : (h + 1) * p.chans] for h in range(wide)], axis=0
        )
        f_s = split(f_rows)
        inner = dot3(f_s, chan_rows_s)
        chan_acc[...] += dot3(ct_s, f_s, TN)
        for h, k in enumerate(ks):
            inner_ref[pl.ds(k, p.pairs, stride=p.times), :] = paired(inner[h * r1 : (h + 1) * r1])

    def outer(q, carry):
        for s in range(slots):
            step = q * slots + s
            one(step, s)

            @pl.when(step + slots < steps)
            def _():
                for c in copies(step + slots, s):
                    c.start()

        return carry

    lax.fori_loop(0, steps // slots, outer, 0)

    fit_acc[...] = (dot3(split(sensor_f), split(ggt[...]), TN) - fit_acc[...]) * p.fit_scale
    chan_acc[...] = chan_acc[...] * p.chan_scale
    time_sum = jnp.zeros((r3, p.times), f32)
    for ht, out in enumerate((keep, send)):
        half = lax.bitwise_xor(my_time, ht)
        for m in range(p.n_channel):
            quarter = lax.bitwise_xor(my_chan, m)
            base = m * p.chunk
            for rr in range(p.pairs_part):
                r = (half * p.n_channel + quarter) * p.pairs_part + rr
                rows = pl.ds(pl.multiple_of(r * p.times, p.times), p.times)
                inner_s = split(inner_ref[rows, :])
                out[base + rr * r3 : base + (rr + 1) * r3, :] = dot3(time_s, inner_s) * p.core_scale
                time_sum = time_sum + dot3(split(core_pair[r]), inner_s, NT)
            chunk = quarter * p.n_time + half
            start = pl.multiple_of(chunk * p.share, 16)
            fit = fit_acc[pl.ds(start, p.share), :]
            out[base + p.sum_rows : base + p.chunk, :] = paired(fit)
        chan_start = pl.multiple_of(half * p.chan_rows, 8)
        out[p.n_channel * p.chunk : p.rows, :] = chan_acc[pl.ds(chan_start, p.chan_rows), :]
    time_acc[...] = jnp.zeros_like(time_acc)
    time_acc[:, 0 : p.times] = time_sum * p.time_scale
    for m in range(p.n_channel):
        quarter = lax.bitwise_xor(my_chan, m)
        base = m * p.chunk + p.core_rows
        start = pl.multiple_of(quarter * p.time_rows, 8)
        keep[base : base + p.time_rows, :] = time_acc[pl.ds(start, p.time_rows), :]
        send[base : base + p.time_rows, :] = jnp.zeros((p.time_rows, LANES), f32)


def partials(p, place, tensor, core, sensor_t, chan_t, time_t):
    wide, slots = 4, 4
    tall = 256
    width = wide * p.chans
    out = jax.ShapeDtypeStruct((p.rows, LANES), f32)
    return pl.pallas_call(
        functools.partial(partial_kernel, p, wide, slots, tall),
        in_specs=[smem, anywhere, vmem, vmem, vmem, vmem],
        out_specs=[vmem, vmem],
        out_shape=[out, out],
        scratch_shapes=[
            pltpu.VMEM((slots, p.sensors, width), f32),
            pltpu.SemaphoreType.DMA((slots, wide)),
            pltpu.VMEM((p.pairs, p.r3, 2 * p.r2), f32),
            pltpu.VMEM((p.pairs * p.times, 2 * p.r2), f32),
            pltpu.VMEM((p.pairs * p.times, 2 * p.r2), f32),
            pltpu.VMEM((p.sensors, p.r1), f32),
            pltpu.VMEM((p.r2, p.chans), f32),
            pltpu.VMEM((p.r3, LANES), f32),
            pltpu.VMEM((p.r1, p.r1), f32),
            pltpu.VMEM((2 * p.r1, p.sensors), bf16),
        ],
        compiler_params=pltpu.CompilerParams(vmem_limit_bytes=56 * 2**20),
        cost_estimate=pl.CostEstimate(
            flops=12 * p.sensors * p.r1 * p.times * p.chans,
            bytes_accessed=4 * p.sensors * p.times * p.chans,
            transcendentals=0,
        ),
        name="partials",
    )(place, tensor, core, sensor_t, chan_t, time_t)


def graph_kernel(
    p, piece, slots,
    place, ids, edges, gathered, fit, out_t, weights, near, own, sem,
):
    block = edges.shape[-1]
    pieces = p.share // piece
    blocks = p.sensors // block
    first = place[2] * pieces

    def copies(g):
        at = first + g
        b = at // (block // piece)
        off = pl.multiple_of((at % (block // piece)) * piece, piece)
        moves = [pltpu.make_async_copy(edges.at[b, :, pl.ds(off, piece), :], weights.at[g], sem.at[g, 0])]
        for n in range(slots):
            other = ids[b, n]
            shard = lax.bitwise_xor(other // blocks, place[3])
            lanes = pl.ds(pl.multiple_of((other % blocks) * block, block), block)
            moves.append(
                pltpu.make_async_copy(gathered.at[shard, :, lanes], near.at[g, n], sem.at[g, 1 + n])
            )
        lanes = pl.ds(pl.multiple_of(b * block, block), block)
        moves.append(pltpu.make_async_copy(gathered.at[0, :, lanes], own.at[g], sem.at[g, 1 + slots]))
        return moves, off

    for g in range(pieces):
        for c in copies(g)[0]:
            c.start()
    parts = []
    for g in range(pieces):
        moves, off = copies(g)
        for c in moves:
            c.wait()
        pulled = jnp.zeros((piece, 2 * p.r1), f32)
        degree = jnp.zeros((piece, 1), f32)
        for n in range(slots):
            w = weights[g, n].astype(f32)
            degree = degree + jnp.sum(w, axis=1, keepdims=True)
            near_h, near_l = split(near[g, n])
            pulled = pulled + dot(w.astype(bf16), jnp.concatenate([near_h, near_l], axis=0), NT)
        near_rows = own[g].T
        rows = jnp.zeros((piece, p.r1), f32)
        for k in range(block // piece):
            rows = jnp.where(off == k * piece, near_rows[k * piece : (k + 1) * piece], rows)
        parts.append(lap_weight * (degree * rows - (pulled[:, : p.r1] + pulled[:, p.r1 :])))
    graph = jnp.concatenate(parts, axis=0)
    out_t[...] = (graph + halves(fit[...])).T


def graph_rows(p, place, ids, edges, gathered, fit):
    block = edges.shape[-1]
    slots = edges.shape[1]
    piece = math.gcd(p.share, block)
    pieces = p.share // piece
    return pl.pallas_call(
        functools.partial(graph_kernel, p, piece, slots),
        in_specs=[smem, smem, anywhere, anywhere, vmem],
        out_specs=vmem,
        out_shape=jax.ShapeDtypeStruct((p.r1, p.share), f32),
        scratch_shapes=[
            pltpu.VMEM((pieces, slots, piece, block), jnp.int32),
            pltpu.VMEM((pieces, slots, p.r1, block), f32),
            pltpu.VMEM((pieces, p.r1, block), f32),
            pltpu.SemaphoreType.DMA((pieces, 2 + slots)),
        ],
        compiler_params=pltpu.CompilerParams(vmem_limit_bytes=32 * 2**20),
        cost_estimate=pl.CostEstimate(flops=10**8, bytes_accessed=10**6, transcendentals=0),
        name="graph",
    )(place, ids, edges, gathered, fit)


def finish_kernel(p, place, *refs):
    own, others, far = refs[0], refs[1 : p.n_channel], refs[p.n_channel]
    core_out, chan_out, time_out = refs[p.n_channel + 1 :]
    my_time, my_chan = place[0], place[1]
    for ht in range(p.n_time):
        half = lax.bitwise_xor(my_time, ht)
        for m in range(p.n_channel):
            quarter = lax.bitwise_xor(my_chan, m)
            for rr in range(p.pairs_part):
                r = (half * p.n_channel + quarter) * p.pairs_part + rr
                if ht == 0:
                    rows = (own if m == 0 else others[m - 1])[rr * p.r3 : (rr + 1) * p.r3, :]
                else:
                    at = m * p.core_rows + rr * p.r3
                    rows = far[at : at + p.r3, :]
                core_out[r] = rows[:, : p.r2]
                core_out[r + p.pairs] = rows[:, p.r2 :]
            if ht == 0:
                rows = (own if m == 0 else others[m - 1])[p.core_rows : p.sum_rows, :]
                start = pl.multiple_of(quarter * p.time_rows, 8)
                time_out[pl.ds(start, p.time_rows), :] = rows[:, : p.times]
        start = pl.multiple_of(half * p.chan_rows, 8)
        if ht == 0:
            chan_out[pl.ds(start, p.chan_rows), :] = own[p.sum_rows : p.sum_rows + p.chan_rows, :]
        else:
            at = p.n_channel * p.core_rows
            chan_out[pl.ds(start, p.chan_rows), :] = far[at : at + p.chan_rows, :]


def finish(p, place, *arrays):
    return pl.pallas_call(
        functools.partial(finish_kernel, p),
        in_specs=[smem] + [vmem] * len(arrays),
        out_specs=[vmem] * 3,
        out_shape=[
            jax.ShapeDtypeStruct((p.r1, p.r3, p.r2), f32),
            jax.ShapeDtypeStruct((p.r2, p.chans), f32),
            jax.ShapeDtypeStruct((p.r3, p.times), f32),
        ],
        compiler_params=pltpu.CompilerParams(vmem_limit_bytes=32 * 2**20),
        cost_estimate=pl.CostEstimate(flops=10**6, bytes_accessed=2 * 10**6, transcendentals=0),
        name="finish",
    )(place, *arrays)


def swap(x, axis, size, mask):
    return lax.ppermute(x, axis, [(i, i ^ mask) for i in range(size)])


def on_device(
    tensor, core, sensor_factor, channel_factor, time_factor, neighbour_ids, edge_weights
):
    n_sensor = lax.axis_size("sensor")
    n_channel = lax.axis_size("channel")
    n_time = lax.axis_size("tm")
    p = Plan(tensor.shape, core.shape, n_sensor, n_channel, n_time)
    my_time, my_chan, my_sensor = (lax.axis_index(a) for a in ("tm", "channel", "sensor"))
    place = jnp.stack([my_time, my_chan, my_chan * n_time + my_time, my_sensor]).astype(jnp.int32)

    gathered = sensor_factor.T[None]
    mask = 1
    while mask < n_sensor:
        gathered = jnp.concatenate([gathered, swap(gathered, "sensor", n_sensor, mask)], axis=0)
        mask *= 2

    keep, send = partials(
        p, place, tensor, core.transpose(0, 2, 1), sensor_factor.T, channel_factor.T, time_factor.T
    )
    held = keep + swap(send, "tm", n_time, 1)
    total = held[: p.chunk]
    for m in range(1, n_channel):
        total = total + swap(held[m * p.chunk : (m + 1) * p.chunk], "channel", n_channel, m)
    fit = total[p.sum_rows :]
    total = jnp.concatenate([total[: p.sum_rows], held[n_channel * p.chunk :]], axis=0)
    mask = 1
    while mask < n_sensor:
        total = total + swap(total, "sensor", n_sensor, mask)
        mask *= 2
    others = [
        swap(total[: p.sum_rows], "channel", n_channel, m) for m in range(1, n_channel)
    ]
    near = jnp.concatenate(
        [total[: p.core_rows]] + [o[: p.core_rows] for o in others] + [total[p.sum_rows :]], axis=0
    )
    far = swap(near, "tm", n_time, 1)
    core_t, chan_t, time_t = finish(p, place, total, *others, far)
    sensor_t = graph_rows(p, place, neighbour_ids, edge_weights, gathered, fit)
    return (core_t.transpose(0, 2, 1), sensor_t.T, chan_t.T, time_t.T)


def solution(mesh):
    return jax.shard_map(
        on_device,
        mesh=mesh,
        in_specs=(
            P("sensor", "tm", "channel"),
            P(),
            P("sensor", None),
            P("channel", None),
            P("tm", None),
            P("sensor", None),
            P("sensor", None, None, None),
        ),
        out_specs=(P(), P(("sensor", "channel", "tm"), None), P("channel", None), P("tm", None)),
        check_vma=False,
    )
```

```python
import functools
import math

import jax
import jax.numpy as jnp
from jax import lax
from jax.experimental import pallas as pl
from jax.experimental.pallas import tpu as pltpu
from jax.sharding import PartitionSpec as P

lap_weight = 1.0 / 512.0
f32, bf16 = jnp.float32, jnp.bfloat16
NN = (((1,), (0,)), ((), ()))
NT = (((1,), (1,)), ((), ()))
TN = (((0,), (0,)), ((), ()))
LANES = 128
LAG = False
vmem = pl.BlockSpec(memory_space=pltpu.VMEM)
smem = pl.BlockSpec(memory_space=pltpu.SMEM)
anywhere = pl.BlockSpec(memory_space=pl.ANY)


def split(x):
    high = x.astype(bf16)
    return high, (x - high.astype(f32)).astype(bf16)


def dot(a, b, dims=NN):
    return lax.dot_general(a, b, dims, preferred_element_type=f32)


def dot3(a, b, dims=NN):
    return dot(a[0], b[0], dims) + (dot(a[0], b[1], dims) + dot(a[1], b[0], dims))


def halves(x):
    w = x.shape[1] // 2
    return jnp.concatenate([x[:, :w], x[:, w:]], axis=0)


def paired(x):
    n = x.shape[0] // 2
    return jnp.concatenate([x[:n], x[n:]], axis=1)


class Plan:
    def __init__(self, tensor, core, n_sensor, n_channel, n_time):
        self.sensors, self.times, self.chans = tensor
        self.r1, self.r2, self.r3 = core
        self.n_sensor, self.n_channel, self.n_time = n_sensor, n_channel, n_time
        self.parts = n_channel * n_time
        self.pairs = self.r1 // 2
        self.pairs_part = self.pairs // self.parts
        self.core_rows = self.pairs_part * self.r3
        self.time_rows = self.r3 // n_channel
        self.share = self.sensors // self.parts
        self.fit_rows = self.share // 2
        self.chunk = self.core_rows + self.time_rows + self.fit_rows
        self.sum_rows = self.core_rows + self.time_rows
        self.chan_rows = self.r2 // n_time
        self.rows = n_channel * self.chunk + self.chan_rows
        total = (self.sensors * n_sensor, self.times * n_time, self.chans * n_channel)
        self.core_scale = 1.0 / math.sqrt(total[0] * total[1] * total[2])
        self.chan_scale = 1.0 / math.sqrt(total[0] * total[1])
        self.time_scale = 1.0 / math.sqrt(total[0] * total[2])
        self.fit_scale = 1.0 / math.sqrt(total[1] * total[2])


def both(x):
    zero = jnp.zeros_like(x)
    return jnp.concatenate(
        [jnp.concatenate([x, zero], axis=1), jnp.concatenate([zero, x], axis=1)], axis=0
    )


def partial_kernel(
    p, group, wide, slots, tall,
    x_hbm, core, sensor_t, chan_t, time_t, keep, send,
    buf, sem, core_pair, ct, inner_ref, fit_acc, chan_acc, time_acc, sensor_s,
    fold, g_both, g_parts,
):
    r1, r2, r3 = p.r1, p.r2, p.r3
    width = wide * p.chans
    steps = p.times // wide
    groups = p.times // group
    inside = group // wide
    my_time, my_chan = lax.axis_index("tm"), lax.axis_index("channel")

    def copies(at, slot):
        return [
            pltpu.make_async_copy(
                x_hbm.at[:, at * group + h, :],
                buf.at[slot, :, h * p.chans : (h + 1) * p.chans],
                sem.at[slot, h],
            )
            for h in range(group)
        ]

    for s in range(slots):
        for c in copies(s, s):
            c.start()

    time_s = split(time_t[...])
    for r in range(p.pairs):
        pair = jnp.concatenate([core[r], core[r + p.pairs]], axis=1)
        pair_h, pair_l = split(pair)
        core_pair[r] = jnp.concatenate([pair_h, pair_l, pair_h], axis=1)
        ct[r * p.times : (r + 1) * p.times, :] = dot3(time_s, (pair_h, pair_l), TN)
    chan_h, chan_l = split(both(chan_t[...]))
    chan_twice = jnp.concatenate([chan_h, chan_h], axis=0)
    rows_h, rows_l = split(both(chan_t[...].T))
    rows_parts = jnp.concatenate([rows_h, rows_l], axis=1)
    sensor_f = sensor_t[...]
    sensor_h, sensor_l = split(sensor_f)
    sensor_s[0:r1, :] = sensor_h
    sensor_s[r1 : 2 * r1, :] = sensor_l
    gram_h, gram_l = split(dot3((sensor_h, sensor_l), (sensor_h, sensor_l), NT))
    gram_twice = jnp.concatenate([gram_h, gram_h], axis=1)
    fit_acc[...] = jnp.zeros_like(fit_acc)

    def ct_rows(step):
        at = [ct[pl.ds(step * wide + h, p.pairs, stride=p.times), :] for h in range(wide)]
        return split(jnp.concatenate(at, axis=0))

    def before(step):
        ct_h, ct_l = ct_rows(step)
        g = dot(jnp.concatenate([ct_h, ct_l], axis=1), chan_twice) + dot(ct_h, chan_l)
        g_h, g_l = split(
            jnp.concatenate(
                [halves(g[h * p.pairs : (h + 1) * p.pairs]) for h in range(wide)], axis=1
            )
        )
        g_hl = jnp.concatenate([g_h, g_l], axis=0)
        g_parts[:, step * width : (step + 1) * width] = g_hl
        for h in range(wide):
            at = slice(h * p.chans, (h + 1) * p.chans)
            g_both[step, at, :] = g_hl[:, at].T

    def read(step, slot):
        lanes = slice(step % inside * width, (step % inside + 1) * width)
        g_hl = g_parts[:, step * width : (step + 1) * width]
        folded = dot(gram_twice, g_hl) + dot(gram_l, g_hl[:r1])
        g = g_both[step]
        for i in range(0, p.sensors, tall):
            x_h, x_l = split(buf[slot, i : i + tall, lanes])
            fit_acc[i : i + tall, :] += dot(x_h, g) + dot(x_l, g)
            a = dot(sensor_s[:, i : i + tall], x_h)
            folded = folded - (a[:r1] + a[r1:] + dot(sensor_s[0:r1, i : i + tall], x_l))
        fold[step] = folded

    def after(step, chan_sum):
        folded = fold[step]
        rows = jnp.concatenate(
            [paired(folded[:, h * p.chans : (h + 1) * p.chans]) for h in range(wide)], axis=0
        )
        f_h, f_l = split(rows)
        inner = dot(f_h, rows_parts)
        inner = inner[:, : 2 * r2] + inner[:, 2 * r2 :] + dot(f_l, rows_h)
        for h in range(wide):
            inner_ref[pl.ds(step * wide + h, p.pairs, stride=p.times), :] = inner[h * p.pairs : (h + 1) * p.pairs]
        return chan_sum + dot3(ct_rows(step), (f_h, f_l), TN)

    for step in range(steps):
        before(step)
    chan_sum = jnp.zeros((2 * r2, 2 * p.chans), f32)
    for at in range(groups):
        slot = at % slots
        for c in copies(at, slot):
            c.wait()
        for step in range(at * inside, (at + 1) * inside):
            read(step, slot)
        if at + slots < groups:
            for c in copies(at + slots, slot):
                c.start()
        if LAG and at >= 1:
            for step in range((at - 1) * inside, at * inside):
                chan_sum = after(step, chan_sum)
    for step in range((groups - 1) * inside if LAG else 0, steps):
        chan_sum = after(step, chan_sum)

    ggt = dot(g_parts[...], g_parts[...], NT)
    ggt = ggt[:r1, :r1] + ggt[:r1, r1:] + ggt[r1:, :r1]
    rebuilt = dot3((sensor_h, sensor_l), split(ggt), TN)
    fit_acc[:, :r1] = (rebuilt - (fit_acc[:, :r1] + fit_acc[:, r1:])) * p.fit_scale
    chan_acc[...] = (chan_sum[:r2, : p.chans] + chan_sum[r2:, p.chans :]) * p.chan_scale
    time_h, time_l = time_s
    time_parts = jnp.concatenate([time_h, time_l, time_h], axis=1)
    time_sum = jnp.zeros((r3, p.times), f32)
    for ht, out in enumerate((keep, send)):
        half = lax.bitwise_xor(my_time, ht)
        for m in range(p.n_channel):
            quarter = lax.bitwise_xor(my_chan, m)
            base = m * p.chunk
            for rr in range(p.pairs_part):
                r = (half * p.n_channel + quarter) * p.pairs_part + rr
                rows = pl.ds(pl.multiple_of(r * p.times, p.times), p.times)
                in_h, in_l = split(inner_ref[rows, :])
                out[base + rr * r3 : base + (rr + 1) * r3, :] = (
                    dot(time_parts, jnp.concatenate([in_h, in_h, in_l], axis=0)) * p.core_scale
                )
                time_sum = time_sum + dot(core_pair[r], jnp.concatenate([in_h, in_h, in_l], axis=1), NT)
            chunk = quarter * p.n_time + half
            start = pl.multiple_of(chunk * p.share, 16)
            fit = fit_acc[pl.ds(start, p.share), 0:r1]
            out[base + p.sum_rows : base + p.chunk, :] = paired(fit)
        chan_start = pl.multiple_of(half * p.chan_rows, 8)
        out[p.n_channel * p.chunk : p.rows, :] = chan_acc[pl.ds(chan_start, p.chan_rows), :]
    time_acc[...] = jnp.zeros_like(time_acc)
    time_acc[:, 0 : p.times] = time_sum * p.time_scale
    for m in range(p.n_channel):
        quarter = lax.bitwise_xor(my_chan, m)
        base = m * p.chunk + p.core_rows
        start = pl.multiple_of(quarter * p.time_rows, 8)
        keep[base : base + p.time_rows, :] = time_acc[pl.ds(start, p.time_rows), :]
        send[base : base + p.time_rows, :] = jnp.zeros((p.time_rows, LANES), f32)


def partials(p, tensor, core, sensor_t, chan_t, time_t):
    group, wide, tall = 16, 4, 256
    slots = max(2, min(p.times // group, 2**25 // (4 * p.sensors * group * p.chans)))
    width = wide * p.chans
    out = jax.ShapeDtypeStruct((p.rows, LANES), f32)
    return pl.pallas_call(
        functools.partial(partial_kernel, p, group, wide, slots, tall),
        in_specs=[anywhere, vmem, vmem, vmem, vmem],
        out_specs=[vmem, vmem],
        out_shape=[out, out],
        scratch_shapes=[
            pltpu.VMEM((slots, p.sensors, group * p.chans), f32),
            pltpu.SemaphoreType.DMA((slots, group)),
            pltpu.VMEM((p.pairs, p.r3, 6 * p.r2), bf16),
            pltpu.VMEM((p.pairs * p.times, 2 * p.r2), f32),
            pltpu.VMEM((p.pairs * p.times, 2 * p.r2), f32),
            pltpu.VMEM((p.sensors, 2 * p.r1), f32),
            pltpu.VMEM((p.r2, p.chans), f32),
            pltpu.VMEM((p.r3, LANES), f32),
            pltpu.VMEM((2 * p.r1, p.sensors), bf16),
            pltpu.VMEM((p.times // wide, p.r1, width), f32),
            pltpu.VMEM((p.times // wide, width, 2 * p.r1), bf16),
            pltpu.VMEM((2 * p.r1, p.times * p.chans), bf16),
        ],
        compiler_params=pltpu.CompilerParams(vmem_limit_bytes=56 * 2**20),
        cost_estimate=pl.CostEstimate(
            flops=12 * p.sensors * p.r1 * p.times * p.chans,
            bytes_accessed=4 * p.sensors * p.times * p.chans,
            transcendentals=0,
        ),
        name="partials",
    )(tensor, core, sensor_t, chan_t, time_t)


def graph_kernel(p, piece, ids, edges, *refs):
    shards, (out, weights, near, sem) = refs[: p.n_sensor], refs[p.n_sensor :]
    slots, block = edges.shape[1], edges.shape[-1]
    in_block = block // piece
    pieces = p.share // piece
    blocks = p.sensors // block
    me = lax.axis_index("sensor")
    first = (lax.axis_index("channel") * p.n_time + lax.axis_index("tm")) * pieces

    def where(g):
        at = first + g
        return at // in_block, pl.multiple_of((at % in_block) * piece, piece)

    def edge_copy(g):
        b, off = where(g)
        return pltpu.make_async_copy(edges.at[b, :, pl.ds(off, piece), :], weights.at[g], sem.at[g, slots + 1])

    def block_copy(g, n, shard, at):
        lanes = pl.ds(pl.multiple_of(at * block, block), block)
        return pltpu.make_async_copy(shards[shard].at[:, lanes], near.at[g, :, n * block : (n + 1) * block], sem.at[g, n])

    for g in range(pieces):
        edge_copy(g).start()
        b, _ = where(g)
        block_copy(g, slots, 0, b).start()
        for n in range(slots):
            other = ids[b, n]
            rel = lax.bitwise_xor(other // blocks, me)
            for s in range(p.n_sensor):

                @pl.when(rel == s)
                def _():
                    block_copy(g, n, s, other % blocks).start()

    rows = lax.broadcasted_iota(jnp.int32, (piece, block), 0)
    cols = lax.broadcasted_iota(jnp.int32, (piece, block), 1)
    parts = []
    for g in range(pieces):
        _, off = where(g)
        edge_copy(g).wait()
        for n in range(slots + 1):
            block_copy(g, n, 0, 0).wait()
        w = [weights[g, n].astype(f32) for n in range(slots)]
        degree = jnp.sum(sum(w[1:], w[0]), axis=1, keepdims=True)
        own_h, own_l = split(jnp.where(cols == rows + off, degree, 0.0))
        left = jnp.concatenate([(-x).astype(bf16) for x in w] + [own_h, own_l], axis=1)
        high, low = split(near[g])
        right = jnp.concatenate([high, low], axis=0)
        right = jnp.concatenate([right, right[:, slots * block :]], axis=1)
        term = dot(left, right, NT)
        parts.append((term[:, : p.r1] + term[:, p.r1 :]) * lap_weight)
    out[...] = jnp.concatenate(parts, axis=0).T


def graph_rows(p, ids, edges, *shards):
    block, slots = edges.shape[-1], edges.shape[1]
    piece = math.gcd(p.share, block)
    pieces = p.share // piece
    return pl.pallas_call(
        functools.partial(graph_kernel, p, piece),
        in_specs=[smem] + [anywhere] * (1 + p.n_sensor),
        out_specs=vmem,
        out_shape=jax.ShapeDtypeStruct((p.r1, p.share), f32),
        scratch_shapes=[
            pltpu.VMEM((pieces, slots, piece, block), jnp.int32),
            pltpu.VMEM((pieces, p.r1, (slots + 1) * block), f32),
            pltpu.SemaphoreType.DMA((pieces, slots + 2)),
        ],
        compiler_params=pltpu.CompilerParams(vmem_limit_bytes=32 * 2**20),
        cost_estimate=pl.CostEstimate(flops=10**8, bytes_accessed=10**6, transcendentals=0),
        name="graph",
    )(ids, edges, *shards)


def put_half(p, ht, arrays, core_out, chan_out, core_buf, sem):
    half = lax.bitwise_xor(lax.axis_index("tm"), ht)
    copies = []
    for m in range(p.n_channel):
        for rr in range(p.pairs_part):
            rows = arrays[m][rr * p.r3 : (rr + 1) * p.r3, :]
            core_buf[m, 0, rr] = rows[:, : p.r2]
            core_buf[m, 1, rr] = rows[:, p.r2 :]
        first = (half * p.n_channel + lax.bitwise_xor(lax.axis_index("channel"), m)) * p.pairs_part
        for side in range(2):
            copies.append(
                pltpu.make_async_copy(
                    core_buf.at[m, side],
                    core_out.at[pl.ds(first + side * p.pairs, p.pairs_part)],
                    sem.at[m, side],
                )
            )
            copies[-1].start()
    start = pl.multiple_of(half * p.chan_rows, 8)
    chan_rows = arrays[0].at[p.sum_rows : p.sum_rows + p.chan_rows, :]
    copies.append(
        pltpu.make_async_copy(chan_rows, chan_out.at[pl.ds(start, p.chan_rows), :], sem.at[p.n_channel, 0])
    )
    copies[-1].start()
    return copies


def first_kernel(p, *refs):
    arrays, refs = refs[: p.n_channel], refs[p.n_channel :]
    fit, graph, core_out, chan_out, sensor_out, time_out, core_buf, sem = refs
    copies = put_half(p, 0, arrays, core_out, chan_out, core_buf, sem)
    sensor_out[...] = halves(fit[...]).T + graph[...]
    for m in range(p.n_channel):
        quarter = lax.bitwise_xor(lax.axis_index("channel"), m)
        start = pl.multiple_of(quarter * p.time_rows, 8)
        time_out[pl.ds(start, p.time_rows), :] = arrays[m][p.core_rows : p.sum_rows, : p.times]
    for c in copies:
        c.wait()


def second_kernel(p, *refs):
    arrays, (core_out, chan_out, core_buf, sem) = refs[: p.n_channel], refs[p.n_channel + 2 :]
    for c in put_half(p, 1, arrays, core_out, chan_out, core_buf, sem):
        c.wait()


def half_scratch(p):
    return [
        pltpu.VMEM((p.n_channel, 2, p.pairs_part, p.r3, p.r2), f32),
        pltpu.SemaphoreType.DMA((p.n_channel + 1, 2)),
    ]


def first_half(p, fit, graph, *arrays):
    return pl.pallas_call(
        functools.partial(first_kernel, p),
        in_specs=[vmem] * (len(arrays) + 2),
        out_specs=[anywhere] * 2 + [vmem] * 2,
        out_shape=[
            jax.ShapeDtypeStruct((p.r1, p.r3, p.r2), f32),
            jax.ShapeDtypeStruct((p.r2, p.chans), f32),
            jax.ShapeDtypeStruct((p.r1, p.share), f32),
            jax.ShapeDtypeStruct((p.r3, p.times), f32),
        ],
        scratch_shapes=half_scratch(p),
        compiler_params=pltpu.CompilerParams(vmem_limit_bytes=8 * 2**20),
        cost_estimate=pl.CostEstimate(flops=10**6, bytes_accessed=10**6, transcendentals=0),
        name="first_half",
    )(*arrays, fit, graph)


def second_half(p, core_t, chan_t, *arrays):
    return pl.pallas_call(
        functools.partial(second_kernel, p),
        in_specs=[vmem] * len(arrays) + [anywhere] * 2,
        out_specs=[anywhere] * 2,
        out_shape=[jax.ShapeDtypeStruct(core_t.shape, f32), jax.ShapeDtypeStruct(chan_t.shape, f32)],
        scratch_shapes=half_scratch(p),
        input_output_aliases={len(arrays): 0, len(arrays) + 1: 1},
        compiler_params=pltpu.CompilerParams(vmem_limit_bytes=8 * 2**20),
        cost_estimate=pl.CostEstimate(flops=10**6, bytes_accessed=10**6, transcendentals=0),
        name="second_half",
    )(*arrays, core_t, chan_t)


def swap(x, axis, size, mask):
    return lax.ppermute(x, axis, [(i, i ^ mask) for i in range(size)])


def on_device(
    tensor, core, sensor_factor, channel_factor, time_factor, neighbour_ids, edge_weights
):
    n_sensor = lax.axis_size("sensor")
    n_channel = lax.axis_size("channel")
    n_time = lax.axis_size("tm")
    p = Plan(tensor.shape, core.shape, n_sensor, n_channel, n_time)

    shards = [swap(sensor_factor.T, "sensor", n_sensor, m) for m in range(1, n_sensor)]
    keep, send = partials(
        p, tensor, core.transpose(0, 2, 1), sensor_factor.T, channel_factor.T, time_factor.T
    )
    keep, send, *shards = lax.optimization_barrier((keep, send, *shards))
    held = keep + swap(send, "tm", n_time, 1)
    total = held[: p.chunk]
    for m in range(1, n_channel):
        total = total + swap(held[m * p.chunk : (m + 1) * p.chunk], "channel", n_channel, m)
    graph = graph_rows(p, neighbour_ids, edge_weights, sensor_factor.T, *shards)
    total, graph = lax.optimization_barrier((total, graph))
    fit = total[p.sum_rows :]
    total = jnp.concatenate([total[: p.sum_rows], held[n_channel * p.chunk :]], axis=0)
    for n in range(n_sensor.bit_length() - 1):
        total = total + swap(total, "sensor", n_sensor, 1 << n)
    others = [
        swap(total[: p.sum_rows], "channel", n_channel, m) for m in range(1, n_channel)
    ]
    far = [swap(x, "tm", n_time, 1) for x in (total, *others)]
    core_t, chan_t, sensor_t, time_t = first_half(p, fit, graph, total, *others)
    core_t, chan_t = second_half(p, core_t, chan_t, *far)
    return (core_t.transpose(0, 2, 1), sensor_t.T, chan_t.T, time_t.T)


def solution(mesh):
    return jax.shard_map(
        on_device,
        mesh=mesh,
        in_specs=(
            P("sensor", "tm", "channel"),
            P(),
            P("sensor", None),
            P("channel", None),
            P("tm", None),
            P("sensor", None),
            P("sensor", None, None, None),
        ),
        out_specs=(P(), P(("sensor", "channel", "tm"), None), P("channel", None), P("tm", None)),
        check_vma=False,
    )
```

```python
import functools
import math

import jax
import jax.numpy as jnp
from jax import lax
from jax.experimental import pallas as pl
from jax.experimental.pallas import tpu as pltpu
from jax.sharding import PartitionSpec as P

lap_weight = 1.0 / 512.0
f32, bf16 = jnp.float32, jnp.bfloat16
NN = (((1,), (0,)), ((), ()))
NT = (((1,), (1,)), ((), ()))
TN = (((0,), (0,)), ((), ()))
LANES = 128
BEFORE = 16
vmem = pl.BlockSpec(memory_space=pltpu.VMEM)
smem = pl.BlockSpec(memory_space=pltpu.SMEM)
anywhere = pl.BlockSpec(memory_space=pl.ANY)


def split(x):
    high = x.astype(bf16)
    return high, (x - high.astype(f32)).astype(bf16)


def dot(a, b, dims=NN):
    return lax.dot_general(a, b, dims, preferred_element_type=f32)


def dot3(a, b, dims=NN):
    return dot(a[0], b[0], dims) + (dot(a[0], b[1], dims) + dot(a[1], b[0], dims))


def halves(x):
    w = x.shape[1] // 2
    return jnp.concatenate([x[:, :w], x[:, w:]], axis=0)


def paired(x):
    n = x.shape[0] // 2
    return jnp.concatenate([x[:n], x[n:]], axis=1)


class Plan:
    def __init__(self, tensor, core, n_sensor, n_channel, n_time):
        self.sensors, self.times, self.chans = tensor
        self.r1, self.r2, self.r3 = core
        self.n_sensor, self.n_channel, self.n_time = n_sensor, n_channel, n_time
        self.parts = n_channel * n_time
        self.pairs = self.r1 // 2
        self.pairs_part = self.pairs // self.parts
        self.core_rows = self.pairs_part * self.r3
        self.time_rows = self.r3 // n_channel
        self.share = self.sensors // self.parts
        self.fit_rows = self.share // 2
        self.chunk = self.core_rows + self.time_rows + self.fit_rows
        self.sum_rows = self.core_rows + self.time_rows
        self.chan_rows = self.r2 // n_time
        self.rows = n_channel * self.chunk + self.chan_rows
        total = (self.sensors * n_sensor, self.times * n_time, self.chans * n_channel)
        self.core_scale = 1.0 / math.sqrt(total[0] * total[1] * total[2])
        self.chan_scale = 1.0 / math.sqrt(total[0] * total[1])
        self.time_scale = 1.0 / math.sqrt(total[0] * total[2])
        self.fit_scale = 1.0 / math.sqrt(total[1] * total[2])


def both(x):
    zero = jnp.zeros_like(x)
    return jnp.concatenate(
        [jnp.concatenate([x, zero], axis=1), jnp.concatenate([zero, x], axis=1)], axis=0
    )


def partial_kernel(
    p, groups, wide, tall,
    x_hbm, core_hbm, sensor_hbm, chan_hbm, time_hbm, *refs,
):
    keep, send, refs = refs[0], refs[1], refs[2:]
    buf, sem, core, sensor_t, chan_t, time_t, small_sem, core_turned, ct, inner_ref, fit_acc, chan_acc, time_acc, sensor_s = refs[:14]
    fold, g_both, g_parts = refs[14:]
    r1, r2, r3 = p.r1, p.r2, p.r3
    width = wide * p.chans
    steps = p.times // wide
    my_time, my_chan = lax.axis_index("tm"), lax.axis_index("channel")

    def copies(at):
        first, count, place, _ = groups[at]
        return [
            pltpu.make_async_copy(
                x_hbm.at[:, first + h, :],
                buf.at[:, (place + h) * p.chans : (place + h + 1) * p.chans],
                sem.at[place + h],
            )
            for h in range(count)
        ]

    pairs = ((sensor_hbm, sensor_t), (chan_hbm, chan_t), (time_hbm, time_t), (core_hbm, core))
    small = [pltpu.make_async_copy(a, b, small_sem.at[n]) for n, (a, b) in enumerate(pairs)]
    for c in small:
        c.start()
    behind = {g[3] for g in groups}
    for at in range(len(groups)):
        if at not in behind:
            for c in copies(at):
                c.start()

    for c in small[:3]:
        c.wait()
    time_s = split(time_t[...])
    time_rows_s = split(time_t[...].T)
    chan_h, chan_l = split(both(chan_t[...]))
    chan_twice = jnp.concatenate([chan_h, chan_h], axis=0)
    rows_h, rows_l = split(both(chan_t[...].T))
    rows_parts = jnp.concatenate([rows_h, rows_l], axis=1)
    sensor_h, sensor_l = split(sensor_t[...])
    sensor_s[0:r1, :] = sensor_h
    sensor_s[r1 : 2 * r1, :] = sensor_l
    gram_h, gram_l = split(dot3((sensor_h, sensor_l), (sensor_h, sensor_l), NT))
    gram_twice = jnp.concatenate([gram_h, gram_h], axis=1)

    small[3].wait()
    for first in range(0, p.pairs, p.pairs_part):
        pairs = []
        for r in range(first, first + p.pairs_part):
            pairs.append(jnp.concatenate([core[r], core[r + p.pairs]], axis=1))
            turned_h, turned_l = split(pairs[-1].T)
            core_turned[r] = jnp.concatenate([turned_h, turned_l], axis=1)
        product = dot3(time_rows_s, split(jnp.concatenate(pairs, axis=1)))
        for n in range(p.pairs_part):
            rows = slice((first + n) * p.times, (first + n + 1) * p.times)
            ct[rows, :] = product[:, n * 2 * r2 : (n + 1) * 2 * r2]

    def ct_rows(first, count):
        at = [ct[pl.ds(k, p.pairs, stride=p.times), :] for k in range(first, first + count)]
        return split(jnp.concatenate(at, axis=0))

    def before(first, count):
        ct_h, ct_l = ct_rows(first, count)
        g = dot(jnp.concatenate([ct_h, ct_l], axis=1), chan_twice) + dot(ct_h, chan_l)
        g_h, g_l = split(
            jnp.concatenate(
                [halves(g[h * p.pairs : (h + 1) * p.pairs]) for h in range(count)], axis=1
            )
        )
        g_hl = jnp.concatenate([g_h, g_l], axis=0)
        g_parts[:, first * p.chans : (first + count) * p.chans] = g_hl
        for h in range(count):
            at = slice((first + h) * p.chans, (first + h + 1) * p.chans)
            g_both[at, :] = g_hl[:, h * p.chans : (h + 1) * p.chans].T

    def read(step, place):
        lanes = slice(place * p.chans, place * p.chans + width)
        g_hl = g_parts[:, step * width : (step + 1) * width]
        folded = dot(gram_twice, g_hl) + dot(gram_l, g_hl[:r1])
        g = g_both[step * width : (step + 1) * width, :]
        for i in range(0, p.sensors, tall):
            x_h, x_l = split(buf[i : i + tall, lanes])
            fit_acc[i : i + tall, :] += dot(x_h, g) + dot(x_l, g)
            a = dot(sensor_s[:, i : i + tall], x_h)
            folded = folded - (a[:r1] + a[r1:] + dot(sensor_s[0:r1, i : i + tall], x_l))
        fold[step] = folded

    def after(first, count, chan_sum):
        rows = []
        for step in range(first // wide, (first + count) // wide):
            folded = fold[step]
            rows.extend(paired(folded[:, h * p.chans : (h + 1) * p.chans]) for h in range(wide))
        f_h, f_l = split(jnp.concatenate(rows, axis=0))
        inner = dot(f_h, rows_parts)
        inner = inner[:, : 2 * r2] + inner[:, 2 * r2 :] + dot(f_l, rows_h)
        for h in range(count):
            inner_ref[pl.ds(first + h, p.pairs, stride=p.times), :] = inner[h * p.pairs : (h + 1) * p.pairs]
        return chan_sum + dot3(ct_rows(first, count), (f_h, f_l), TN)

    for first in range(0, p.times, BEFORE):
        before(first, BEFORE)
    ggt = dot(g_parts[...], g_both[...])
    ggt = ggt[:r1, :r1] + ggt[:r1, r1:] + ggt[r1:, :r1]
    fit_acc[:, :r1] = -(dot3(split(ggt), (sensor_h, sensor_l)).T)
    fit_acc[:, r1:] = jnp.zeros((p.sensors, r1), f32)

    chan_sum = jnp.zeros((2 * r2, 2 * p.chans), f32)
    for at, (first, count, place, start_next) in enumerate(groups):
        for c in copies(at):
            c.wait()
        mine = range(first // wide, (first + count) // wide)
        for n, step in enumerate(mine):
            read(step, place + n * wide)
        if start_next is not None:
            for c in copies(start_next):
                c.start()
        if at > 0:
            chan_sum = after(*groups[at - 1][:2], chan_sum)
    chan_sum = after(*groups[-1][:2], chan_sum)

    chan_acc[...] = (chan_sum[:r2, : p.chans] + chan_sum[r2:, p.chans :]) * p.chan_scale
    time_h, time_l = time_s
    time_parts = jnp.concatenate([time_h, time_l, time_h], axis=1)
    time_sum = jnp.zeros((p.times, 2 * r3), f32)
    time_low = jnp.zeros((p.times, r3), f32)
    for ht, out in enumerate((keep, send)):
        half = lax.bitwise_xor(my_time, ht)
        for m in range(p.n_channel):
            quarter = lax.bitwise_xor(my_chan, m)
            base = m * p.chunk
            first = (half * p.n_channel + quarter) * p.pairs_part
            inner = [
                inner_ref[pl.ds(pl.multiple_of((first + n) * p.times, p.times), p.times), :]
                for n in range(p.pairs_part)
            ]
            in_h, in_l = split(jnp.concatenate(inner, axis=1))
            rows = dot(time_parts, jnp.concatenate([in_h, in_h, in_l], axis=0)) * p.core_scale
            for n in range(p.pairs_part):
                out[base + n * r3 : base + (n + 1) * r3, :] = rows[:, n * 2 * r2 : (n + 1) * 2 * r2]
            turned = jnp.concatenate([core_turned[first + n] for n in range(p.pairs_part)], axis=0)
            time_sum = time_sum + dot(in_h, turned)
            time_low = time_low + dot(in_l, turned[:, :r3])
            start = pl.multiple_of((quarter * p.n_time + half) * p.share, 16)
            fit = fit_acc[pl.ds(start, p.share), :]
            out[base + p.sum_rows : base + p.chunk, :] = paired((fit[:, :r1] + fit[:, r1:]) * -p.fit_scale)
        chan_start = pl.multiple_of(half * p.chan_rows, 8)
        out[p.n_channel * p.chunk : p.rows, :] = chan_acc[pl.ds(chan_start, p.chan_rows), :]
    time_acc[...] = jnp.zeros_like(time_acc)
    time_acc[:, 0 : p.times] = (time_sum[:, :r3] + time_sum[:, r3:] + time_low).T * p.time_scale
    for m in range(p.n_channel):
        quarter = lax.bitwise_xor(my_chan, m)
        base = m * p.chunk + p.core_rows
        start = pl.multiple_of(quarter * p.time_rows, 8)
        keep[base : base + p.time_rows, :] = time_acc[pl.ds(start, p.time_rows), :]
        send[base : base + p.time_rows, :] = jnp.zeros((p.time_rows, LANES), f32)


def partials(p, tensor, core, sensor_t, chan_t, time_t):
    wide, tall, unit = 4, 256, 16
    width = wide * p.chans
    if 4 * p.sensors * p.times * p.chans <= 2**25:
        sizes, places = [8, 16, 16, 16, 8], p.times
        assert sum(sizes) == p.times
        groups = [(sum(sizes[:n]), size, sum(sizes[:n]), None) for n, size in enumerate(sizes)]
    else:
        count = p.times // unit
        places = 2 * unit
        groups = [(n * unit, unit, n % 2 * unit, n + 2 if n + 2 < count else None) for n in range(count)]
    return pl.pallas_call(
        functools.partial(partial_kernel, p, groups, wide, tall),
        in_specs=[anywhere] * 5,
        out_specs=[vmem] * 2,
        out_shape=[jax.ShapeDtypeStruct((p.rows, LANES), f32)] * 2,
        scratch_shapes=[
            pltpu.VMEM((p.sensors, places * p.chans), f32),
            pltpu.SemaphoreType.DMA((places,)),
            pltpu.VMEM((p.r1, p.r3, p.r2), f32),
            pltpu.VMEM(sensor_t.shape, f32),
            pltpu.VMEM(chan_t.shape, f32),
            pltpu.VMEM(time_t.shape, f32),
            pltpu.SemaphoreType.DMA((4,)),
            pltpu.VMEM((p.pairs, 2 * p.r2, 2 * p.r3), bf16),
            pltpu.VMEM((p.pairs * p.times, 2 * p.r2), f32),
            pltpu.VMEM((p.pairs * p.times, 2 * p.r2), f32),
            pltpu.VMEM((p.sensors, 2 * p.r1), f32),
            pltpu.VMEM((p.r2, p.chans), f32),
            pltpu.VMEM((p.r3, LANES), f32),
            pltpu.VMEM((2 * p.r1, p.sensors), bf16),
            pltpu.VMEM((p.times // wide, p.r1, width), f32),
            pltpu.VMEM((p.times * p.chans, 2 * p.r1), bf16),
            pltpu.VMEM((2 * p.r1, p.times * p.chans), bf16),
        ],
        compiler_params=pltpu.CompilerParams(vmem_limit_bytes=56 * 2**20),
        cost_estimate=pl.CostEstimate(
            flops=12 * p.sensors * p.r1 * p.times * p.chans,
            bytes_accessed=4 * p.sensors * p.times * p.chans,
            transcendentals=0,
        ),
        name="partials",
    )(tensor, core, sensor_t, chan_t, time_t)


def graph_kernel(p, piece, ids, edges, *refs):
    shards, (out, weights, near, sem) = refs[: p.n_sensor], refs[p.n_sensor :]
    slots, block = edges.shape[1], edges.shape[-1]
    in_block = block // piece
    pieces = p.share // piece
    blocks = p.sensors // block
    me = lax.axis_index("sensor")
    first = (lax.axis_index("channel") * p.n_time + lax.axis_index("tm")) * pieces

    def where(g):
        at = first + g
        return at // in_block, pl.multiple_of((at % in_block) * piece, piece)

    def edge_copy(g):
        b, off = where(g)
        return pltpu.make_async_copy(edges.at[b, :, pl.ds(off, piece), :], weights.at[g], sem.at[g, slots + 1])

    def block_copy(g, n, shard, at):
        lanes = pl.ds(pl.multiple_of(at * block, block), block)
        return pltpu.make_async_copy(shards[shard].at[:, lanes], near.at[g, :, n * block : (n + 1) * block], sem.at[g, n])

    for g in range(pieces):
        edge_copy(g).start()
        b, _ = where(g)
        block_copy(g, slots, 0, b).start()
        for n in range(slots):
            other = ids[b, n]
            rel = lax.bitwise_xor(other // blocks, me)
            for s in range(p.n_sensor):

                @pl.when(rel == s)
                def _():
                    block_copy(g, n, s, other % blocks).start()

    rows = lax.broadcasted_iota(jnp.int32, (piece, block), 0)
    cols = lax.broadcasted_iota(jnp.int32, (piece, block), 1)
    parts = []
    for g in range(pieces):
        _, off = where(g)
        edge_copy(g).wait()
        for n in range(slots + 1):
            block_copy(g, n, 0, 0).wait()
        w = [weights[g, n].astype(f32) for n in range(slots)]
        degree = jnp.sum(sum(w[1:], w[0]), axis=1, keepdims=True)
        own_h, own_l = split(jnp.where(cols == rows + off, degree, 0.0))
        left = jnp.concatenate([(-x).astype(bf16) for x in w] + [own_h, own_l], axis=1)
        high, low = split(near[g])
        right = jnp.concatenate([high, low], axis=0)
        right = jnp.concatenate([right, right[:, slots * block :]], axis=1)
        term = dot(left, right, NT)
        parts.append((term[:, : p.r1] + term[:, p.r1 :]) * lap_weight)
    out[...] = jnp.concatenate(parts, axis=0).T


def graph_rows(p, ids, edges, *shards):
    block, slots = edges.shape[-1], edges.shape[1]
    piece = math.gcd(p.share, block)
    pieces = p.share // piece
    return pl.pallas_call(
        functools.partial(graph_kernel, p, piece),
        in_specs=[smem] + [anywhere] * (1 + p.n_sensor),
        out_specs=vmem,
        out_shape=jax.ShapeDtypeStruct((p.r1, p.share), f32),
        scratch_shapes=[
            pltpu.VMEM((pieces, slots, piece, block), jnp.int32),
            pltpu.VMEM((pieces, p.r1, (slots + 1) * block), f32),
            pltpu.SemaphoreType.DMA((pieces, slots + 2)),
        ],
        compiler_params=pltpu.CompilerParams(vmem_limit_bytes=32 * 2**20),
        cost_estimate=pl.CostEstimate(flops=10**8, bytes_accessed=10**6, transcendentals=0),
        name="graph",
    )(ids, edges, *shards)


def put_half(p, ht, arrays, core_out, chan_out, core_buf, sem):
    half = lax.bitwise_xor(lax.axis_index("tm"), ht)
    copies = []
    for m in range(p.n_channel):
        for rr in range(p.pairs_part):
            rows = arrays[m][rr * p.r3 : (rr + 1) * p.r3, :]
            core_buf[m, 0, rr] = rows[:, : p.r2]
            core_buf[m, 1, rr] = rows[:, p.r2 :]
        first = (half * p.n_channel + lax.bitwise_xor(lax.axis_index("channel"), m)) * p.pairs_part
        for side in range(2):
            copies.append(
                pltpu.make_async_copy(
                    core_buf.at[m, side],
                    core_out.at[pl.ds(first + side * p.pairs, p.pairs_part)],
                    sem.at[m, side],
                )
            )
            copies[-1].start()
    start = pl.multiple_of(half * p.chan_rows, 8)
    chan_rows = arrays[0].at[p.sum_rows : p.sum_rows + p.chan_rows, :]
    copies.append(
        pltpu.make_async_copy(chan_rows, chan_out.at[pl.ds(start, p.chan_rows), :], sem.at[p.n_channel, 0])
    )
    copies[-1].start()
    return copies


def first_kernel(p, *refs):
    arrays, refs = refs[: p.n_channel], refs[p.n_channel :]
    fit, graph, core_out, chan_out, sensor_out, time_out, core_buf, sem = refs
    copies = put_half(p, 0, arrays, core_out, chan_out, core_buf, sem)
    sensor_out[...] = halves(fit[...]).T + graph[...]
    for m in range(p.n_channel):
        quarter = lax.bitwise_xor(lax.axis_index("channel"), m)
        start = pl.multiple_of(quarter * p.time_rows, 8)
        time_out[pl.ds(start, p.time_rows), :] = arrays[m][p.core_rows : p.sum_rows, : p.times]
    for c in copies:
        c.wait()


def second_kernel(p, *refs):
    arrays, (core_out, chan_out, core_buf, sem) = refs[: p.n_channel], refs[p.n_channel + 2 :]
    for c in put_half(p, 1, arrays, core_out, chan_out, core_buf, sem):
        c.wait()


def half_scratch(p):
    return [
        pltpu.VMEM((p.n_channel, 2, p.pairs_part, p.r3, p.r2), f32),
        pltpu.SemaphoreType.DMA((p.n_channel + 1, 2)),
    ]


def first_half(p, fit, graph, *arrays):
    return pl.pallas_call(
        functools.partial(first_kernel, p),
        in_specs=[vmem] * (len(arrays) + 2),
        out_specs=[anywhere] * 2 + [vmem] * 2,
        out_shape=[
            jax.ShapeDtypeStruct((p.r1, p.r3, p.r2), f32),
            jax.ShapeDtypeStruct((p.r2, p.chans), f32),
            jax.ShapeDtypeStruct((p.r1, p.share), f32),
            jax.ShapeDtypeStruct((p.r3, p.times), f32),
        ],
        scratch_shapes=half_scratch(p),
        compiler_params=pltpu.CompilerParams(vmem_limit_bytes=8 * 2**20),
        cost_estimate=pl.CostEstimate(flops=10**6, bytes_accessed=10**6, transcendentals=0),
        name="first_half",
    )(*arrays, fit, graph)


def second_half(p, core_t, chan_t, *arrays):
    return pl.pallas_call(
        functools.partial(second_kernel, p),
        in_specs=[vmem] * len(arrays) + [anywhere] * 2,
        out_specs=[anywhere] * 2,
        out_shape=[jax.ShapeDtypeStruct(core_t.shape, f32), jax.ShapeDtypeStruct(chan_t.shape, f32)],
        scratch_shapes=half_scratch(p),
        input_output_aliases={len(arrays): 0, len(arrays) + 1: 1},
        compiler_params=pltpu.CompilerParams(vmem_limit_bytes=8 * 2**20),
        cost_estimate=pl.CostEstimate(flops=10**6, bytes_accessed=10**6, transcendentals=0),
        name="second_half",
    )(*arrays, core_t, chan_t)


def swap(x, axis, size, mask):
    return lax.ppermute(x, axis, [(i, i ^ mask) for i in range(size)])


def on_device(
    tensor, core, sensor_factor, channel_factor, time_factor, neighbour_ids, edge_weights
):
    n_sensor = lax.axis_size("sensor")
    n_channel = lax.axis_size("channel")
    n_time = lax.axis_size("tm")
    p = Plan(tensor.shape, core.shape, n_sensor, n_channel, n_time)

    shards = [swap(sensor_factor.T, "sensor", n_sensor, m) for m in range(1, n_sensor)]
    keep, send = partials(
        p, tensor, core.transpose(0, 2, 1), sensor_factor.T, channel_factor.T, time_factor.T
    )
    keep, send, *shards = lax.optimization_barrier((keep, send, *shards))
    held = keep + swap(send, "tm", n_time, 1)
    total = held[: p.chunk]
    for m in range(1, n_channel):
        total = total + swap(held[m * p.chunk : (m + 1) * p.chunk], "channel", n_channel, m)
    graph = graph_rows(p, neighbour_ids, edge_weights, sensor_factor.T, *shards)
    total, graph = lax.optimization_barrier((total, graph))
    fit = total[p.sum_rows :]
    total = jnp.concatenate([total[: p.sum_rows], held[n_channel * p.chunk :]], axis=0)
    for n in range(n_sensor.bit_length() - 1):
        total = total + swap(total, "sensor", n_sensor, 1 << n)
    others = [
        swap(total[: p.sum_rows], "channel", n_channel, m) for m in range(1, n_channel)
    ]
    far = [swap(x, "tm", n_time, 1) for x in (total, *others)]
    core_t, chan_t, sensor_t, time_t = first_half(p, fit, graph, total, *others)
    core_t, chan_t = second_half(p, core_t, chan_t, *far)
    return (core_t.transpose(0, 2, 1), sensor_t.T, chan_t.T, time_t.T)


def solution(mesh):
    return jax.shard_map(
        on_device,
        mesh=mesh,
        in_specs=(
            P("sensor", "tm", "channel"),
            P(),
            P("sensor", None),
            P("channel", None),
            P("tm", None),
            P("sensor", None),
            P("sensor", None, None, None),
        ),
        out_specs=(P(), P(("sensor", "channel", "tm"), None), P("channel", None), P("tm", None)),
        check_vma=False,
    )
```

```python
import functools
import math

import jax
import jax.numpy as jnp
from jax import lax
from jax.experimental import pallas as pl
from jax.experimental.pallas import tpu as pltpu
from jax.sharding import PartitionSpec as P

lap_weight = 1.0 / 512.0
f32, bf16 = jnp.float32, jnp.bfloat16
NN = (((1,), (0,)), ((), ()))
NT = (((1,), (1,)), ((), ()))
TN = (((0,), (0,)), ((), ()))
LANES = 128
BEFORE = 16
vmem = pl.BlockSpec(memory_space=pltpu.VMEM)
smem = pl.BlockSpec(memory_space=pltpu.SMEM)
anywhere = pl.BlockSpec(memory_space=pl.ANY)


def split(x):
    high = x.astype(bf16)
    return high, (x - high.astype(f32)).astype(bf16)


def dot(a, b, dims=NN):
    return lax.dot_general(a, b, dims, preferred_element_type=f32)


def dot3(a, b, dims=NN):
    return dot(a[0], b[0], dims) + (dot(a[0], b[1], dims) + dot(a[1], b[0], dims))


def halves(x):
    w = x.shape[1] // 2
    return jnp.concatenate([x[:, :w], x[:, w:]], axis=0)


def paired(x):
    n = x.shape[0] // 2
    return jnp.concatenate([x[:n], x[n:]], axis=1)


class Plan:
    def __init__(self, tensor, core, n_sensor, n_channel, n_time):
        self.sensors, self.times, self.chans = tensor
        self.r1, self.r2, self.r3 = core
        self.n_sensor, self.n_channel, self.n_time = n_sensor, n_channel, n_time
        self.parts = n_channel * n_time
        self.pairs = self.r1 // 2
        self.pairs_part = self.pairs // self.parts
        self.core_rows = self.pairs_part * self.r3
        self.time_rows = self.r3 // n_channel
        self.share = self.sensors // self.parts
        self.fit_rows = self.share // 2
        self.chunk = self.core_rows + self.time_rows + self.fit_rows
        self.sum_rows = self.core_rows + self.time_rows
        self.chan_rows = self.r2 // n_time
        self.rows = n_channel * self.chunk + self.chan_rows
        total = (self.sensors * n_sensor, self.times * n_time, self.chans * n_channel)
        self.core_scale = 1.0 / math.sqrt(total[0] * total[1] * total[2])
        self.chan_scale = 1.0 / math.sqrt(total[0] * total[1])
        self.time_scale = 1.0 / math.sqrt(total[0] * total[2])
        self.fit_scale = 1.0 / math.sqrt(total[1] * total[2])


def both(x):
    zero = jnp.zeros_like(x)
    return jnp.concatenate(
        [jnp.concatenate([x, zero], axis=1), jnp.concatenate([zero, x], axis=1)], axis=0
    )


def partial_kernel(
    p, groups, wide, tall,
    x_hbm, core_hbm, sensor_hbm, chan_hbm, time_hbm, *refs,
):
    keep, send, refs = refs[0], refs[1], refs[2:]
    buf, sem, core, sensor_t, chan_t, time_t, small_sem, core_turned, ct, inner_ref, fit_acc, chan_acc, time_acc, sensor_s = refs[:14]
    fold, g_both, g_parts = refs[14:]
    r1, r2, r3 = p.r1, p.r2, p.r3
    width = wide * p.chans
    steps = p.times // wide
    my_time, my_chan = lax.axis_index("tm"), lax.axis_index("channel")

    def copies(at):
        first, count, place, _ = groups[at]
        return [
            pltpu.make_async_copy(
                x_hbm.at[:, first + h, :],
                buf.at[:, (place + h) * p.chans : (place + h + 1) * p.chans],
                sem.at[place + h],
            )
            for h in range(count)
        ]

    pairs = ((sensor_hbm, sensor_t), (chan_hbm, chan_t), (time_hbm, time_t), (core_hbm, core))
    small = [pltpu.make_async_copy(a, b, small_sem.at[n]) for n, (a, b) in enumerate(pairs)]
    for c in small:
        c.start()
    behind = {g[3] for g in groups}
    for at in range(len(groups)):
        if at not in behind:
            for c in copies(at):
                c.start()

    for c in small[:3]:
        c.wait()
    time_s = split(time_t[...])
    time_rows_s = split(time_t[...].T)
    chan_h, chan_l = split(both(chan_t[...]))
    chan_twice = jnp.concatenate([chan_h, chan_h], axis=0)
    rows_h, rows_l = split(both(chan_t[...].T))
    rows_parts = jnp.concatenate([rows_h, rows_l], axis=1)
    sensor_h, sensor_l = split(sensor_t[...])
    sensor_s[0:r1, :] = sensor_h
    sensor_s[r1 : 2 * r1, :] = sensor_l
    gram_h, gram_l = split(dot3((sensor_h, sensor_l), (sensor_h, sensor_l), NT))
    gram = jnp.concatenate([gram_h, gram_h, gram_l], axis=1)

    small[3].wait()
    for first in range(0, p.pairs, p.pairs_part):
        pairs = []
        for r in range(first, first + p.pairs_part):
            pairs.append(jnp.concatenate([core[r], core[r + p.pairs]], axis=1))
            turned_h, turned_l = split(pairs[-1].T)
            core_turned[r] = jnp.concatenate([turned_h, turned_l], axis=1)
        product = dot3(time_rows_s, split(jnp.concatenate(pairs, axis=1)))
        for n in range(p.pairs_part):
            rows = slice((first + n) * p.times, (first + n + 1) * p.times)
            ct[rows, :] = product[:, n * 2 * r2 : (n + 1) * 2 * r2]

    def ct_rows(first, count):
        at = [ct[pl.ds(k, p.pairs, stride=p.times), :] for k in range(first, first + count)]
        return split(jnp.concatenate(at, axis=0))

    def before(first, count):
        ct_h, ct_l = ct_rows(first, count)
        g = dot(jnp.concatenate([ct_h, ct_l], axis=1), chan_twice) + dot(ct_h, chan_l)
        g_h, g_l = split(
            jnp.concatenate(
                [halves(g[h * p.pairs : (h + 1) * p.pairs]) for h in range(count)], axis=1
            )
        )
        g_hl = jnp.concatenate([g_h, g_l], axis=0)
        g_parts[:, first * p.chans : (first + count) * p.chans] = g_hl
        for h in range(count):
            at = slice((first + h) * p.chans, (first + h + 1) * p.chans)
            g_both[at, :] = g_hl[:, h * p.chans : (h + 1) * p.chans].T

    def read(step, place):
        lanes = slice(place * p.chans, place * p.chans + width)
        g_hl = g_parts[:, step * width : (step + 1) * width]
        folded = dot(gram, jnp.concatenate([g_hl, g_hl[:r1]], axis=0))
        g = g_both[step * width : (step + 1) * width, :]
        for i in range(0, p.sensors, tall):
            x_h, x_l = split(buf[i : i + tall, lanes])
            fit_acc[i : i + tall, :] += dot(x_h, g) + dot(x_l, g)
            a = dot(sensor_s[:, i : i + tall], x_h)
            folded = folded - (a[:r1] + a[r1:] + dot(sensor_s[0:r1, i : i + tall], x_l))
        fold[step] = folded

    def after(first, count, chan_sum):
        rows = []
        for step in range(first // wide, (first + count) // wide):
            folded = fold[step]
            rows.extend(paired(folded[:, h * p.chans : (h + 1) * p.chans]) for h in range(wide))
        f_h, f_l = split(jnp.concatenate(rows, axis=0))
        inner = dot(f_h, rows_parts)
        inner = inner[:, : 2 * r2] + inner[:, 2 * r2 :] + dot(f_l, rows_h)
        for h in range(count):
            inner_ref[pl.ds(first + h, p.pairs, stride=p.times), :] = inner[h * p.pairs : (h + 1) * p.pairs]
        ct_h, ct_l = (c.T for c in ct_rows(first, count))
        return chan_sum + dot3((ct_h, ct_l), (f_h, f_l))

    for first in range(0, p.times, BEFORE):
        before(first, BEFORE)
    ggt = dot(g_parts[...], g_both[...])
    ggt = ggt[:r1, :r1] + ggt[:r1, r1:] + ggt[r1:, :r1]
    fit_acc[:, :r1] = -(dot3(split(ggt), (sensor_h, sensor_l)).T)
    fit_acc[:, r1:] = jnp.zeros((p.sensors, r1), f32)

    chan_sum = jnp.zeros((2 * r2, 2 * p.chans), f32)
    for at, (first, count, place, start_next) in enumerate(groups):
        for c in copies(at):
            c.wait()
        mine = range(first // wide, (first + count) // wide)
        for n, step in enumerate(mine):
            read(step, place + n * wide)
        if start_next is not None:
            for c in copies(start_next):
                c.start()
        if at > 0:
            chan_sum = after(*groups[at - 1][:2], chan_sum)
    chan_sum = after(*groups[-1][:2], chan_sum)

    chan_acc[...] = (chan_sum[:r2, : p.chans] + chan_sum[r2:, p.chans :]) * p.chan_scale
    time_h, time_l = time_s
    time_parts = jnp.concatenate([time_h, time_l, time_h], axis=1)
    time_sum = jnp.zeros((p.times, 2 * r3), f32)
    time_low = jnp.zeros((p.times, r3), f32)
    for ht, out in enumerate((keep, send)):
        half = lax.bitwise_xor(my_time, ht)
        for m in range(p.n_channel):
            quarter = lax.bitwise_xor(my_chan, m)
            base = m * p.chunk
            first = (half * p.n_channel + quarter) * p.pairs_part
            inner = [
                inner_ref[pl.ds(pl.multiple_of((first + n) * p.times, p.times), p.times), :]
                for n in range(p.pairs_part)
            ]
            in_h, in_l = split(jnp.concatenate(inner, axis=1))
            rows = dot(time_parts, jnp.concatenate([in_h, in_h, in_l], axis=0)) * p.core_scale
            for n in range(p.pairs_part):
                out[base + n * r3 : base + (n + 1) * r3, :] = rows[:, n * 2 * r2 : (n + 1) * 2 * r2]
            turned = jnp.concatenate([core_turned[first + n] for n in range(p.pairs_part)], axis=0)
            time_sum = time_sum + dot(in_h, turned)
            time_low = time_low + dot(in_l, turned[:, :r3])
            start = pl.multiple_of((quarter * p.n_time + half) * p.share, 16)
            fit = fit_acc[pl.ds(start, p.share), :]
            out[base + p.sum_rows : base + p.chunk, :] = paired((fit[:, :r1] + fit[:, r1:]) * -p.fit_scale)
        chan_start = pl.multiple_of(half * p.chan_rows, 8)
        out[p.n_channel * p.chunk : p.rows, :] = chan_acc[pl.ds(chan_start, p.chan_rows), :]
    time_acc[...] = jnp.zeros_like(time_acc)
    time_acc[:, 0 : p.times] = (time_sum[:, :r3] + time_sum[:, r3:] + time_low).T * p.time_scale
    for m in range(p.n_channel):
        quarter = lax.bitwise_xor(my_chan, m)
        base = m * p.chunk + p.core_rows
        start = pl.multiple_of(quarter * p.time_rows, 8)
        keep[base : base + p.time_rows, :] = time_acc[pl.ds(start, p.time_rows), :]
        send[base : base + p.time_rows, :] = jnp.zeros((p.time_rows, LANES), f32)


def partials(p, tensor, core, sensor_t, chan_t, time_t):
    wide, tall, unit = 4, 256, 16
    width = wide * p.chans
    if 4 * p.sensors * p.times * p.chans <= 2**25:
        sizes, places = [8, 16, 16, 16, 8], p.times
        assert sum(sizes) == p.times
        groups = [(sum(sizes[:n]), size, sum(sizes[:n]), None) for n, size in enumerate(sizes)]
    else:
        count = p.times // unit
        places = 2 * unit
        groups = [(n * unit, unit, n % 2 * unit, n + 2 if n + 2 < count else None) for n in range(count)]
    return pl.pallas_call(
        functools.partial(partial_kernel, p, groups, wide, tall),
        in_specs=[anywhere] * 5,
        out_specs=[vmem] * 2,
        out_shape=[jax.ShapeDtypeStruct((p.rows, LANES), f32)] * 2,
        scratch_shapes=[
            pltpu.VMEM((p.sensors, places * p.chans), f32),
            pltpu.SemaphoreType.DMA((places,)),
            pltpu.VMEM((p.r1, p.r3, p.r2), f32),
            pltpu.VMEM(sensor_t.shape, f32),
            pltpu.VMEM(chan_t.shape, f32),
            pltpu.VMEM(time_t.shape, f32),
            pltpu.SemaphoreType.DMA((4,)),
            pltpu.VMEM((p.pairs, 2 * p.r2, 2 * p.r3), bf16),
            pltpu.VMEM((p.pairs * p.times, 2 * p.r2), f32),
            pltpu.VMEM((p.pairs * p.times, 2 * p.r2), f32),
            pltpu.VMEM((p.sensors, 2 * p.r1), f32),
            pltpu.VMEM((p.r2, p.chans), f32),
            pltpu.VMEM((p.r3, LANES), f32),
            pltpu.VMEM((2 * p.r1, p.sensors), bf16),
            pltpu.VMEM((p.times // wide, p.r1, width), f32),
            pltpu.VMEM((p.times * p.chans, 2 * p.r1), bf16),
            pltpu.VMEM((2 * p.r1, p.times * p.chans), bf16),
        ],
        compiler_params=pltpu.CompilerParams(vmem_limit_bytes=56 * 2**20),
        cost_estimate=pl.CostEstimate(
            flops=12 * p.sensors * p.r1 * p.times * p.chans,
            bytes_accessed=4 * p.sensors * p.times * p.chans,
            transcendentals=0,
        ),
        name="partials",
    )(tensor, core, sensor_t, chan_t, time_t)


def graph_kernel(p, piece, ids, edges, *refs):
    shards, (out, weights, near, sem) = refs[: p.n_sensor], refs[p.n_sensor :]
    slots, block = edges.shape[1], edges.shape[-1]
    in_block = block // piece
    pieces = p.share // piece
    blocks = p.sensors // block
    me = lax.axis_index("sensor")
    first = (lax.axis_index("channel") * p.n_time + lax.axis_index("tm")) * pieces

    def where(g):
        at = first + g
        return at // in_block, pl.multiple_of((at % in_block) * piece, piece)

    def edge_copy(g):
        b, off = where(g)
        return pltpu.make_async_copy(edges.at[b, :, pl.ds(off, piece), :], weights.at[g], sem.at[g, slots + 1])

    def block_copy(g, n, shard, at):
        lanes = pl.ds(pl.multiple_of(at * block, block), block)
        return pltpu.make_async_copy(shards[shard].at[:, lanes], near.at[g, :, n * block : (n + 1) * block], sem.at[g, n])

    for g in range(pieces):
        edge_copy(g).start()
        b, _ = where(g)
        block_copy(g, slots, 0, b).start()
        for n in range(slots):
            other = ids[b, n]
            rel = lax.bitwise_xor(other // blocks, me)
            for s in range(p.n_sensor):

                @pl.when(rel == s)
                def _():
                    block_copy(g, n, s, other % blocks).start()

    rows = lax.broadcasted_iota(jnp.int32, (piece, block), 0)
    cols = lax.broadcasted_iota(jnp.int32, (piece, block), 1)
    parts = []
    for g in range(pieces):
        _, off = where(g)
        edge_copy(g).wait()
        for n in range(slots + 1):
            block_copy(g, n, 0, 0).wait()
        w = [weights[g, n].astype(f32) for n in range(slots)]
        degree = jnp.sum(sum(w[1:], w[0]), axis=1, keepdims=True)
        own_h, own_l = split(jnp.where(cols == rows + off, degree, 0.0))
        left = jnp.concatenate([(-x).astype(bf16) for x in w] + [own_h, own_l], axis=1)
        high, low = split(near[g])
        right = jnp.concatenate([high, low], axis=0)
        right = jnp.concatenate([right, right[:, slots * block :]], axis=1)
        term = dot(left, right, NT)
        parts.append((term[:, : p.r1] + term[:, p.r1 :]) * lap_weight)
    out[...] = jnp.concatenate(parts, axis=0).T


def graph_rows(p, ids, edges, *shards):
    block, slots = edges.shape[-1], edges.shape[1]
    piece = math.gcd(p.share, block)
    pieces = p.share // piece
    return pl.pallas_call(
        functools.partial(graph_kernel, p, piece),
        in_specs=[smem] + [anywhere] * (1 + p.n_sensor),
        out_specs=vmem,
        out_shape=jax.ShapeDtypeStruct((p.r1, p.share), f32),
        scratch_shapes=[
            pltpu.VMEM((pieces, slots, piece, block), jnp.int32),
            pltpu.VMEM((pieces, p.r1, (slots + 1) * block), f32),
            pltpu.SemaphoreType.DMA((pieces, slots + 2)),
        ],
        compiler_params=pltpu.CompilerParams(vmem_limit_bytes=32 * 2**20),
        cost_estimate=pl.CostEstimate(flops=10**8, bytes_accessed=10**6, transcendentals=0),
        name="graph",
    )(ids, edges, *shards)


def put_half(p, ht, arrays, core_out, chan_out, core_buf, sem):
    half = lax.bitwise_xor(lax.axis_index("tm"), ht)
    copies = []
    for m in range(p.n_channel):
        for rr in range(p.pairs_part):
            rows = arrays[m][rr * p.r3 : (rr + 1) * p.r3, :]
            core_buf[m, 0, rr] = rows[:, : p.r2]
            core_buf[m, 1, rr] = rows[:, p.r2 :]
        first = (half * p.n_channel + lax.bitwise_xor(lax.axis_index("channel"), m)) * p.pairs_part
        for side in range(2):
            copies.append(
                pltpu.make_async_copy(
                    core_buf.at[m, side],
                    core_out.at[pl.ds(first + side * p.pairs, p.pairs_part)],
                    sem.at[m, side],
                )
            )
            copies[-1].start()
    start = pl.multiple_of(half * p.chan_rows, 8)
    chan_rows = arrays[0].at[p.sum_rows : p.sum_rows + p.chan_rows, :]
    copies.append(
        pltpu.make_async_copy(chan_rows, chan_out.at[pl.ds(start, p.chan_rows), :], sem.at[p.n_channel, 0])
    )
    copies[-1].start()
    return copies


def first_kernel(p, *refs):
    arrays, refs = refs[: p.n_channel], refs[p.n_channel :]
    fit, graph, core_out, chan_out, sensor_out, time_out, core_buf, sem = refs
    copies = put_half(p, 0, arrays, core_out, chan_out, core_buf, sem)
    sensor_out[...] = halves(fit[...]).T + graph[...]
    for m in range(p.n_channel):
        quarter = lax.bitwise_xor(lax.axis_index("channel"), m)
        start = pl.multiple_of(quarter * p.time_rows, 8)
        time_out[pl.ds(start, p.time_rows), :] = arrays[m][p.core_rows : p.sum_rows, : p.times]
    for c in copies:
        c.wait()


def second_kernel(p, *refs):
    arrays, (core_out, chan_out, core_buf, sem) = refs[: p.n_channel], refs[p.n_channel + 2 :]
    for c in put_half(p, 1, arrays, core_out, chan_out, core_buf, sem):
        c.wait()


def half_scratch(p):
    return [
        pltpu.VMEM((p.n_channel, 2, p.pairs_part, p.r3, p.r2), f32),
        pltpu.SemaphoreType.DMA((p.n_channel + 1, 2)),
    ]


def first_half(p, fit, graph, *arrays):
    return pl.pallas_call(
        functools.partial(first_kernel, p),
        in_specs=[vmem] * (len(arrays) + 2),
        out_specs=[anywhere] * 2 + [vmem] * 2,
        out_shape=[
            jax.ShapeDtypeStruct((p.r1, p.r3, p.r2), f32),
            jax.ShapeDtypeStruct((p.r2, p.chans), f32),
            jax.ShapeDtypeStruct((p.r1, p.share), f32),
            jax.ShapeDtypeStruct((p.r3, p.times), f32),
        ],
        scratch_shapes=half_scratch(p),
        compiler_params=pltpu.CompilerParams(vmem_limit_bytes=8 * 2**20),
        cost_estimate=pl.CostEstimate(flops=10**6, bytes_accessed=10**6, transcendentals=0),
        name="first_half",
    )(*arrays, fit, graph)


def second_half(p, core_t, chan_t, *arrays):
    return pl.pallas_call(
        functools.partial(second_kernel, p),
        in_specs=[vmem] * len(arrays) + [anywhere] * 2,
        out_specs=[anywhere] * 2,
        out_shape=[jax.ShapeDtypeStruct(core_t.shape, f32), jax.ShapeDtypeStruct(chan_t.shape, f32)],
        scratch_shapes=half_scratch(p),
        input_output_aliases={len(arrays): 0, len(arrays) + 1: 1},
        compiler_params=pltpu.CompilerParams(vmem_limit_bytes=8 * 2**20),
        cost_estimate=pl.CostEstimate(flops=10**6, bytes_accessed=10**6, transcendentals=0),
        name="second_half",
    )(*arrays, core_t, chan_t)


def settle(x):
    def body(x_ref, out):
        out[...] = x_ref[...]

    return pl.pallas_call(
        body,
        in_specs=[vmem],
        out_specs=vmem,
        out_shape=jax.ShapeDtypeStruct(x.shape, x.dtype),
        compiler_params=pltpu.CompilerParams(vmem_limit_bytes=4 * 2**20),
        cost_estimate=pl.CostEstimate(flops=10**5, bytes_accessed=10**6, transcendentals=0),
        name="settle",
    )(x)


def swap(x, axis, size, mask):
    return lax.ppermute(x, axis, [(i, i ^ mask) for i in range(size)])


def on_device(
    tensor, core, sensor_factor, channel_factor, time_factor, neighbour_ids, edge_weights
):
    n_sensor = lax.axis_size("sensor")
    n_channel = lax.axis_size("channel")
    n_time = lax.axis_size("tm")
    p = Plan(tensor.shape, core.shape, n_sensor, n_channel, n_time)

    shards = [swap(sensor_factor.T, "sensor", n_sensor, m) for m in range(1, n_sensor)]
    keep, send = partials(
        p, tensor, core.transpose(0, 2, 1), sensor_factor.T, channel_factor.T, time_factor.T
    )
    keep, send, *shards = lax.optimization_barrier((keep, send, *shards))
    held = settle(keep) + swap(send, "tm", n_time, 1)
    total = held[: p.sum_rows]
    for m in range(1, n_channel):
        at = m * p.chunk
        total = total + swap(held[at : at + p.sum_rows], "channel", n_channel, m)
    graph = graph_rows(p, neighbour_ids, edge_weights, sensor_factor.T, *shards)
    total, graph, held = lax.optimization_barrier((total, graph, held))
    fit = held[p.sum_rows : p.chunk]
    for m in range(1, n_channel):
        at = m * p.chunk
        fit = fit + swap(held[at + p.sum_rows : at + p.chunk], "channel", n_channel, m)
    total = jnp.concatenate([total, held[n_channel * p.chunk :]], axis=0)
    for n in range(n_sensor.bit_length() - 1):
        total = total + swap(total, "sensor", n_sensor, 1 << n)
    total, fit = lax.optimization_barrier((total, fit))
    others = [
        swap(total[: p.sum_rows], "channel", n_channel, m) for m in range(1, n_channel)
    ]
    far = [swap(x, "tm", n_time, 1) for x in (total, *others)]
    core_t, chan_t, sensor_t, time_t = first_half(p, fit, graph, total, *others)
    core_t, chan_t = second_half(p, core_t, chan_t, *far)
    return (core_t.transpose(0, 2, 1), sensor_t.T, chan_t.T, time_t.T)


def solution(mesh):
    return jax.shard_map(
        on_device,
        mesh=mesh,
        in_specs=(
            P("sensor", "tm", "channel"),
            P(),
            P("sensor", None),
            P("channel", None),
            P("tm", None),
            P("sensor", None),
            P("sensor", None, None, None),
        ),
        out_specs=(P(), P(("sensor", "channel", "tm"), None), P("channel", None), P("tm", None)),
        check_vma=False,
    )
```

```python
import functools
import math

import jax
import jax.numpy as jnp
from jax import lax
from jax.experimental import pallas as pl
from jax.experimental.pallas import tpu as pltpu
from jax.sharding import PartitionSpec as P

lap_weight = 1.0 / 512.0
f32, bf16 = jnp.float32, jnp.bfloat16
NN = (((1,), (0,)), ((), ()))
NT = (((1,), (1,)), ((), ()))
TN = (((0,), (0,)), ((), ()))
LANES = 128
BEFORE = 16
vmem = pl.BlockSpec(memory_space=pltpu.VMEM)
smem = pl.BlockSpec(memory_space=pltpu.SMEM)
anywhere = pl.BlockSpec(memory_space=pl.ANY)


def split(x):
    high = x.astype(bf16)
    return high, (x - high.astype(f32)).astype(bf16)


def dot(a, b, dims=NN):
    return lax.dot_general(a, b, dims, preferred_element_type=f32)


def dot3(a, b, dims=NN):
    return dot(a[0], b[0], dims) + (dot(a[0], b[1], dims) + dot(a[1], b[0], dims))


def halves(x):
    w = x.shape[1] // 2
    return jnp.concatenate([x[:, :w], x[:, w:]], axis=0)


def paired(x):
    n = x.shape[0] // 2
    return jnp.concatenate([x[:n], x[n:]], axis=1)


class Plan:
    def __init__(self, tensor, core, n_sensor, n_channel, n_time):
        self.sensors, self.times, self.chans = tensor
        self.r1, self.r2, self.r3 = core
        self.n_sensor, self.n_channel, self.n_time = n_sensor, n_channel, n_time
        self.parts = n_channel * n_time
        self.pairs = self.r1 // 2
        self.pairs_part = self.pairs // self.parts
        self.core_rows = self.pairs_part * self.r3
        self.time_rows = self.r3 // n_channel
        self.share = self.sensors // self.parts
        self.fit_rows = self.share // 2
        self.chunk = self.core_rows + self.time_rows + self.fit_rows
        self.sum_rows = self.core_rows + self.time_rows
        self.chan_rows = self.r2 // n_time
        self.rows = n_channel * self.chunk + self.chan_rows
        total = (self.sensors * n_sensor, self.times * n_time, self.chans * n_channel)
        self.core_scale = 1.0 / math.sqrt(total[0] * total[1] * total[2])
        self.chan_scale = 1.0 / math.sqrt(total[0] * total[1])
        self.time_scale = 1.0 / math.sqrt(total[0] * total[2])
        self.fit_scale = 1.0 / math.sqrt(total[1] * total[2])


def both(x):
    zero = jnp.zeros_like(x)
    return jnp.concatenate(
        [jnp.concatenate([x, zero], axis=1), jnp.concatenate([zero, x], axis=1)], axis=0
    )


def partial_kernel(
    p, groups, wide, tall,
    x_hbm, core_hbm, sensor_hbm, chan_hbm, time_hbm, *refs,
):
    keep, send, refs = refs[0], refs[1], refs[2:]
    buf, sem, core, sensor_t, chan_t, time_t, small_sem, core_turned, ct, inner_ref, fit_acc, chan_acc, time_acc, sensor_s = refs[:14]
    fold, g_both, g_parts = refs[14:]
    r1, r2, r3 = p.r1, p.r2, p.r3
    width = wide * p.chans
    steps = p.times // wide
    my_time, my_chan = lax.axis_index("tm"), lax.axis_index("channel")

    def copies(at):
        first, count, place, _ = groups[at]
        return [
            pltpu.make_async_copy(
                x_hbm.at[:, first + h, :],
                buf.at[:, (place + h) * p.chans : (place + h + 1) * p.chans],
                sem.at[place + h],
            )
            for h in range(count)
        ]

    pairs = ((sensor_hbm, sensor_t), (chan_hbm, chan_t), (time_hbm, time_t), (core_hbm, core))
    small = [pltpu.make_async_copy(a, b, small_sem.at[n]) for n, (a, b) in enumerate(pairs)]
    for c in small:
        c.start()
    behind = {g[3] for g in groups}
    for at in range(len(groups)):
        if at not in behind:
            for c in copies(at):
                c.start()

    for c in small[:3]:
        c.wait()
    time_s = split(time_t[...])
    time_rows_s = split(time_t[...].T)
    chan_h, chan_l = split(both(chan_t[...]))
    chan_twice = jnp.concatenate([chan_h, chan_h], axis=0)
    rows_h, rows_l = split(both(chan_t[...].T))
    rows_parts = jnp.concatenate([rows_h, rows_l], axis=1)
    sensor_h, sensor_l = split(sensor_t[...])
    sensor_s[0:r1, :] = sensor_h
    sensor_s[r1 : 2 * r1, :] = sensor_l
    gram_h, gram_l = split(dot3((sensor_h, sensor_l), (sensor_h, sensor_l), NT))
    gram = jnp.concatenate([gram_h, gram_h, gram_l], axis=1)

    small[3].wait()
    for first in range(0, p.pairs, p.pairs_part):
        pairs = []
        for r in range(first, first + p.pairs_part):
            pairs.append(jnp.concatenate([core[r], core[r + p.pairs]], axis=1))
            turned_h, turned_l = split(pairs[-1].T)
            core_turned[r] = jnp.concatenate([turned_h, turned_l], axis=1)
        product = dot3(time_rows_s, split(jnp.concatenate(pairs, axis=1)))
        for n in range(p.pairs_part):
            rows = slice((first + n) * p.times, (first + n + 1) * p.times)
            ct[rows, :] = product[:, n * 2 * r2 : (n + 1) * 2 * r2]

    def ct_rows(first, count):
        at = [ct[pl.ds(k, p.pairs, stride=p.times), :] for k in range(first, first + count)]
        return split(jnp.concatenate(at, axis=0))

    def before(first, count):
        ct_h, ct_l = ct_rows(first, count)
        g = dot(jnp.concatenate([ct_h, ct_l], axis=1), chan_twice) + dot(ct_h, chan_l)
        g_h, g_l = split(
            jnp.concatenate(
                [halves(g[h * p.pairs : (h + 1) * p.pairs]) for h in range(count)], axis=1
            )
        )
        g_hl = jnp.concatenate([g_h, g_l], axis=0)
        g_parts[:, first * p.chans : (first + count) * p.chans] = g_hl
        for h in range(count):
            at = slice((first + h) * p.chans, (first + h + 1) * p.chans)
            g_both[at, :] = g_hl[:, h * p.chans : (h + 1) * p.chans].T

    def read(step, place):
        lanes = slice(place * p.chans, place * p.chans + width)
        g_hl = g_parts[:, step * width : (step + 1) * width]
        folded = dot(gram, jnp.concatenate([g_hl, g_hl[:r1]], axis=0))
        g = g_both[step * width : (step + 1) * width, :]
        for i in range(0, p.sensors, tall):
            x_h, x_l = split(buf[i : i + tall, lanes])
            fit_acc[i : i + tall, :] += dot(x_h, g) + dot(x_l, g)
            a = dot(sensor_s[:, i : i + tall], x_h)
            folded = folded - (a[:r1] + a[r1:] + dot(sensor_s[0:r1, i : i + tall], x_l))
        fold[step] = folded

    def after(first, count, chan_sum):
        rows = []
        for step in range(first // wide, (first + count) // wide):
            folded = fold[step]
            rows.extend(paired(folded[:, h * p.chans : (h + 1) * p.chans]) for h in range(wide))
        f_h, f_l = split(jnp.concatenate(rows, axis=0))
        inner = dot(f_h, rows_parts)
        inner = inner[:, : 2 * r2] + inner[:, 2 * r2 :] + dot(f_l, rows_h)
        for h in range(count):
            inner_ref[pl.ds(first + h, p.pairs, stride=p.times), :] = inner[h * p.pairs : (h + 1) * p.pairs]
        ct_h, ct_l = (c.T for c in ct_rows(first, count))
        return chan_sum + dot3((ct_h, ct_l), (f_h, f_l))

    for first in range(0, p.times, BEFORE):
        before(first, BEFORE)
    ggt = dot(g_parts[...], g_both[...])
    ggt = ggt[:r1, :r1] + ggt[:r1, r1:] + ggt[r1:, :r1]
    fit_acc[:, :r1] = -(dot3(split(ggt), (sensor_h, sensor_l)).T)
    fit_acc[:, r1:] = jnp.zeros((p.sensors, r1), f32)

    chan_sum = jnp.zeros((2 * r2, 2 * p.chans), f32)
    for at, (first, count, place, start_next) in enumerate(groups):
        for c in copies(at):
            c.wait()
        mine = range(first // wide, (first + count) // wide)
        for n, step in enumerate(mine):
            read(step, place + n * wide)
        if start_next is not None:
            for c in copies(start_next):
                c.start()
        if at > 0:
            chan_sum = after(*groups[at - 1][:2], chan_sum)
    chan_sum = after(*groups[-1][:2], chan_sum)

    chan_acc[...] = (chan_sum[:r2, : p.chans] + chan_sum[r2:, p.chans :]) * p.chan_scale
    time_h, time_l = time_s
    time_parts = jnp.concatenate([time_h, time_l, time_h], axis=1)
    time_sum = jnp.zeros((p.times, 2 * r3), f32)
    time_low = jnp.zeros((p.times, r3), f32)
    for ht, out in enumerate((keep, send)):
        half = lax.bitwise_xor(my_time, ht)
        for m in range(p.n_channel):
            quarter = lax.bitwise_xor(my_chan, m)
            base = m * p.chunk
            first = (half * p.n_channel + quarter) * p.pairs_part
            inner = [
                inner_ref[pl.ds(pl.multiple_of((first + n) * p.times, p.times), p.times), :]
                for n in range(p.pairs_part)
            ]
            in_h, in_l = split(jnp.concatenate(inner, axis=1))
            rows = dot(time_parts, jnp.concatenate([in_h, in_h, in_l], axis=0)) * p.core_scale
            for n in range(p.pairs_part):
                out[base + n * r3 : base + (n + 1) * r3, :] = rows[:, n * 2 * r2 : (n + 1) * 2 * r2]
            turned = jnp.concatenate([core_turned[first + n] for n in range(p.pairs_part)], axis=0)
            time_sum = time_sum + dot(in_h, turned)
            time_low = time_low + dot(in_l, turned[:, :r3])
            start = pl.multiple_of((quarter * p.n_time + half) * p.share, 16)
            fit = fit_acc[pl.ds(start, p.share), :]
            out[base + p.sum_rows : base + p.chunk, :] = paired((fit[:, :r1] + fit[:, r1:]) * -p.fit_scale)
        chan_start = pl.multiple_of(half * p.chan_rows, 8)
        out[p.n_channel * p.chunk : p.rows, :] = chan_acc[pl.ds(chan_start, p.chan_rows), :]
    time_acc[...] = jnp.zeros_like(time_acc)
    time_acc[:, 0 : p.times] = (time_sum[:, :r3] + time_sum[:, r3:] + time_low).T * p.time_scale
    for m in range(p.n_channel):
        quarter = lax.bitwise_xor(my_chan, m)
        base = m * p.chunk + p.core_rows
        start = pl.multiple_of(quarter * p.time_rows, 8)
        keep[base : base + p.time_rows, :] = time_acc[pl.ds(start, p.time_rows), :]
        send[base : base + p.time_rows, :] = jnp.zeros((p.time_rows, LANES), f32)


def partials(p, tensor, core, sensor_t, chan_t, time_t):
    wide, tall, unit = 4, 256, 16
    width = wide * p.chans
    if 4 * p.sensors * p.times * p.chans <= 2**25:
        sizes, places = [8, 16, 16, 16, 8], p.times
        assert sum(sizes) == p.times
        groups = [(sum(sizes[:n]), size, sum(sizes[:n]), None) for n, size in enumerate(sizes)]
    else:
        count = p.times // unit
        places = 2 * unit
        groups = [(n * unit, unit, n % 2 * unit, n + 2 if n + 2 < count else None) for n in range(count)]
    return pl.pallas_call(
        functools.partial(partial_kernel, p, groups, wide, tall),
        in_specs=[anywhere] * 5,
        out_specs=[vmem] * 2,
        out_shape=[jax.ShapeDtypeStruct((p.rows, LANES), f32)] * 2,
        scratch_shapes=[
            pltpu.VMEM((p.sensors, places * p.chans), f32),
            pltpu.SemaphoreType.DMA((places,)),
            pltpu.VMEM((p.r1, p.r3, p.r2), f32),
            pltpu.VMEM(sensor_t.shape, f32),
            pltpu.VMEM(chan_t.shape, f32),
            pltpu.VMEM(time_t.shape, f32),
            pltpu.SemaphoreType.DMA((4,)),
            pltpu.VMEM((p.pairs, 2 * p.r2, 2 * p.r3), bf16),
            pltpu.VMEM((p.pairs * p.times, 2 * p.r2), f32),
            pltpu.VMEM((p.pairs * p.times, 2 * p.r2), f32),
            pltpu.VMEM((p.sensors, 2 * p.r1), f32),
            pltpu.VMEM((p.r2, p.chans), f32),
            pltpu.VMEM((p.r3, LANES), f32),
            pltpu.VMEM((2 * p.r1, p.sensors), bf16),
            pltpu.VMEM((p.times // wide, p.r1, width), f32),
            pltpu.VMEM((p.times * p.chans, 2 * p.r1), bf16),
            pltpu.VMEM((2 * p.r1, p.times * p.chans), bf16),
        ],
        compiler_params=pltpu.CompilerParams(vmem_limit_bytes=56 * 2**20),
        cost_estimate=pl.CostEstimate(
            flops=12 * p.sensors * p.r1 * p.times * p.chans,
            bytes_accessed=4 * p.sensors * p.times * p.chans,
            transcendentals=0,
        ),
        name="partials",
    )(tensor, core, sensor_t, chan_t, time_t)


def graph_kernel(p, piece, ids, edges, *refs):
    shards, (out, weights, near, sem) = refs[: p.n_sensor], refs[p.n_sensor :]
    slots, block = edges.shape[1], edges.shape[-1]
    in_block = block // piece
    pieces = p.share // piece
    blocks = p.sensors // block
    me = lax.axis_index("sensor")
    first = (lax.axis_index("channel") * p.n_time + lax.axis_index("tm")) * pieces

    def where(g):
        at = first + g
        return at // in_block, pl.multiple_of((at % in_block) * piece, piece)

    def edge_copy(g):
        b, off = where(g)
        return pltpu.make_async_copy(edges.at[b, :, pl.ds(off, piece), :], weights.at[g], sem.at[g, slots + 1])

    def block_copy(g, n, shard, at):
        lanes = pl.ds(pl.multiple_of(at * block, block), block)
        return pltpu.make_async_copy(shards[shard].at[:, lanes], near.at[g, :, n * block : (n + 1) * block], sem.at[g, n])

    for g in range(pieces):
        edge_copy(g).start()
        b, _ = where(g)
        block_copy(g, slots, 0, b).start()
        for n in range(slots):
            other = ids[b, n]
            rel = lax.bitwise_xor(other // blocks, me)
            for s in range(p.n_sensor):

                @pl.when(rel == s)
                def _():
                    block_copy(g, n, s, other % blocks).start()

    rows = lax.broadcasted_iota(jnp.int32, (piece, block), 0)
    cols = lax.broadcasted_iota(jnp.int32, (piece, block), 1)
    parts = []
    for g in range(pieces):
        _, off = where(g)
        edge_copy(g).wait()
        for n in range(slots + 1):
            block_copy(g, n, 0, 0).wait()
        w = [weights[g, n].astype(f32) for n in range(slots)]
        degree = jnp.sum(sum(w[1:], w[0]), axis=1, keepdims=True)
        own_h, own_l = split(jnp.where(cols == rows + off, degree, 0.0))
        left = jnp.concatenate([(-x).astype(bf16) for x in w] + [own_h, own_l], axis=1)
        high, low = split(near[g])
        right = jnp.concatenate([high, low], axis=0)
        right = jnp.concatenate([right, right[:, slots * block :]], axis=1)
        term = dot(left, right, NT)
        parts.append((term[:, : p.r1] + term[:, p.r1 :]) * lap_weight)
    out[...] = jnp.concatenate(parts, axis=0).T


def graph_rows(p, ids, edges, *shards):
    block, slots = edges.shape[-1], edges.shape[1]
    piece = math.gcd(p.share, block)
    pieces = p.share // piece
    return pl.pallas_call(
        functools.partial(graph_kernel, p, piece),
        in_specs=[smem] + [anywhere] * (1 + p.n_sensor),
        out_specs=vmem,
        out_shape=jax.ShapeDtypeStruct((p.r1, p.share), f32),
        scratch_shapes=[
            pltpu.VMEM((pieces, slots, piece, block), jnp.int32),
            pltpu.VMEM((pieces, p.r1, (slots + 1) * block), f32),
            pltpu.SemaphoreType.DMA((pieces, slots + 2)),
        ],
        compiler_params=pltpu.CompilerParams(vmem_limit_bytes=32 * 2**20),
        cost_estimate=pl.CostEstimate(flops=10**8, bytes_accessed=10**6, transcendentals=0),
        name="graph",
    )(ids, edges, *shards)


def put_half(p, ht, arrays, core_out, chan_out, core_buf, sem):
    half = lax.bitwise_xor(lax.axis_index("tm"), ht)
    copies = []
    for m in range(p.n_channel):
        for rr in range(p.pairs_part):
            rows = arrays[m][rr * p.r3 : (rr + 1) * p.r3, :]
            core_buf[m, 0, rr] = rows[:, : p.r2]
            core_buf[m, 1, rr] = rows[:, p.r2 :]
        first = (half * p.n_channel + lax.bitwise_xor(lax.axis_index("channel"), m)) * p.pairs_part
        for side in range(2):
            copies.append(
                pltpu.make_async_copy(
                    core_buf.at[m, side],
                    core_out.at[pl.ds(first + side * p.pairs, p.pairs_part)],
                    sem.at[m, side],
                )
            )
            copies[-1].start()
    start = pl.multiple_of(half * p.chan_rows, 8)
    chan_rows = arrays[0].at[p.sum_rows : p.sum_rows + p.chan_rows, :]
    copies.append(
        pltpu.make_async_copy(chan_rows, chan_out.at[pl.ds(start, p.chan_rows), :], sem.at[p.n_channel, 0])
    )
    copies[-1].start()
    return copies


def first_kernel(p, *refs):
    arrays, refs = refs[: p.n_channel], refs[p.n_channel :]
    core_out, chan_out, time_out, core_buf, sem = refs
    copies = put_half(p, 0, arrays, core_out, chan_out, core_buf, sem)
    for m in range(p.n_channel):
        quarter = lax.bitwise_xor(lax.axis_index("channel"), m)
        start = pl.multiple_of(quarter * p.time_rows, 8)
        time_out[pl.ds(start, p.time_rows), :] = arrays[m][p.core_rows : p.sum_rows, : p.times]
    for c in copies:
        c.wait()


def second_kernel(p, *refs):
    arrays, (core_out, chan_out, core_buf, sem) = refs[: p.n_channel], refs[p.n_channel + 2 :]
    for c in put_half(p, 1, arrays, core_out, chan_out, core_buf, sem):
        c.wait()


def half_scratch(p):
    return [
        pltpu.VMEM((p.n_channel, 2, p.pairs_part, p.r3, p.r2), f32),
        pltpu.SemaphoreType.DMA((p.n_channel + 1, 2)),
    ]


def sensor_rows(fit, graph):
    def body(fit_ref, graph_ref, out):
        out[...] = halves(fit_ref[...]).T + graph_ref[...]

    return pl.pallas_call(
        body,
        in_specs=[vmem] * 2,
        out_specs=vmem,
        out_shape=jax.ShapeDtypeStruct(graph.shape, f32),
        compiler_params=pltpu.CompilerParams(vmem_limit_bytes=4 * 2**20),
        cost_estimate=pl.CostEstimate(flops=10**5, bytes_accessed=10**5, transcendentals=0),
        name="sensor_rows",
    )(fit, graph)


def first_half(p, *arrays):
    return pl.pallas_call(
        functools.partial(first_kernel, p),
        in_specs=[vmem] * len(arrays),
        out_specs=[anywhere] * 2 + [vmem],
        out_shape=[
            jax.ShapeDtypeStruct((p.r1, p.r3, p.r2), f32),
            jax.ShapeDtypeStruct((p.r2, p.chans), f32),
            jax.ShapeDtypeStruct((p.r3, p.times), f32),
        ],
        scratch_shapes=half_scratch(p),
        compiler_params=pltpu.CompilerParams(vmem_limit_bytes=8 * 2**20),
        cost_estimate=pl.CostEstimate(flops=10**6, bytes_accessed=10**6, transcendentals=0),
        name="first_half",
    )(*arrays)


def second_half(p, core_t, chan_t, *arrays):
    return pl.pallas_call(
        functools.partial(second_kernel, p),
        in_specs=[vmem] * len(arrays) + [anywhere] * 2,
        out_specs=[anywhere] * 2,
        out_shape=[jax.ShapeDtypeStruct(core_t.shape, f32), jax.ShapeDtypeStruct(chan_t.shape, f32)],
        scratch_shapes=half_scratch(p),
        input_output_aliases={len(arrays): 0, len(arrays) + 1: 1},
        compiler_params=pltpu.CompilerParams(vmem_limit_bytes=8 * 2**20),
        cost_estimate=pl.CostEstimate(flops=10**6, bytes_accessed=10**6, transcendentals=0),
        name="second_half",
    )(*arrays, core_t, chan_t)


def settle(x):
    def body(x_ref, out):
        out[...] = x_ref[...]

    return pl.pallas_call(
        body,
        in_specs=[vmem],
        out_specs=vmem,
        out_shape=jax.ShapeDtypeStruct(x.shape, x.dtype),
        compiler_params=pltpu.CompilerParams(vmem_limit_bytes=4 * 2**20),
        cost_estimate=pl.CostEstimate(flops=10**5, bytes_accessed=10**6, transcendentals=0),
        name="settle",
    )(x)


def swap(x, axis, size, mask):
    return lax.ppermute(x, axis, [(i, i ^ mask) for i in range(size)])


def on_device(
    tensor, core, sensor_factor, channel_factor, time_factor, neighbour_ids, edge_weights
):
    n_sensor = lax.axis_size("sensor")
    n_channel = lax.axis_size("channel")
    n_time = lax.axis_size("tm")
    p = Plan(tensor.shape, core.shape, n_sensor, n_channel, n_time)

    shards = [swap(sensor_factor.T, "sensor", n_sensor, m) for m in range(1, n_sensor)]
    keep, send = partials(
        p, tensor, core.transpose(0, 2, 1), sensor_factor.T, channel_factor.T, time_factor.T
    )
    keep, send, *shards = lax.optimization_barrier((keep, send, *shards))
    held = settle(keep) + swap(send, "tm", n_time, 1)
    total = held[: p.sum_rows]
    for m in range(1, n_channel):
        at = m * p.chunk
        total = total + swap(held[at : at + p.sum_rows], "channel", n_channel, m)
    graph = graph_rows(p, neighbour_ids, edge_weights, sensor_factor.T, *shards)
    total, graph, held = lax.optimization_barrier((total, graph, held))
    fit = held[p.sum_rows : p.chunk]
    for m in range(1, n_channel):
        at = m * p.chunk
        fit = fit + swap(held[at + p.sum_rows : at + p.chunk], "channel", n_channel, m)
    total = jnp.concatenate([total, held[n_channel * p.chunk :]], axis=0)
    for n in range(n_sensor.bit_length() - 1):
        total = total + swap(total, "sensor", n_sensor, 1 << n)
    total, sensor_t = lax.optimization_barrier((total, sensor_rows(fit, graph)))
    others = [
        swap(total[: p.sum_rows], "channel", n_channel, m) for m in range(1, n_channel)
    ]
    far = [swap(x, "tm", n_time, 1) for x in (total, *others)]
    core_t, chan_t, time_t = first_half(p, total, *others)
    core_t, chan_t = second_half(p, core_t, chan_t, *far)
    return (core_t.transpose(0, 2, 1), sensor_t.T, chan_t.T, time_t.T)


def solution(mesh):
    return jax.shard_map(
        on_device,
        mesh=mesh,
        in_specs=(
            P("sensor", "tm", "channel"),
            P(),
            P("sensor", None),
            P("channel", None),
            P("tm", None),
            P("sensor", None),
            P("sensor", None, None, None),
        ),
        out_specs=(P(), P(("sensor", "channel", "tm"), None), P("channel", None), P("tm", None)),
        check_vma=False,
    )
```
